32 devices in a mesh: leaf: 4 (over y, core), front: 8 (over z, x).
Axes of the slice: x: 2, y: 2, z: 4, core: 2. Of those that a mesh axis runs over, the one named last changes fastest.
Arguments:
- front_entries: float32 [8, 4, 128, 4, 8, 128], P(None, 'leaf', None, None, 'front'), as said below
- child_panels: bfloat16 [4, 1024, 512], P('leaf', 'front'), may hold values from -0.053955078 to 0.053955078
- child_blocks: bfloat16 [4, 1024, 1024], P('leaf', None, 'front'), as said below
- child_map: int32 [4, 8], replicated, may hold values from 0 to 31, as said below
Outputs:
- factored: float32 [8, 4, 128, 4, 8, 128], P(None, 'leaf', None, None, 'front')
The draws below stay inside these ranges and needn't reach their ends.
Inputs may be any that keep to these rules, and one draw needn't show every extreme that they name: The blocks of one subtree go to distinct parent blocks, and child_map[c, j] modulo 8 equals j. front_entries is symmetric and positive definite, with its diagonal in 6 to 9. `child_blocks`: each subtree's block is symmetric with diagonal in 6 to 9 and small independent entries elsewhere.
All inputs are finite; a program needn't handle non-finite values.
Results may differ from the reference program's by a relative error of at most 0.0012.
Values may be sent and summed in bfloat16 or wider, within the bound.
A program may use at most 128 MiB of HBM per device.

```python
import jax
import jax.numpy as jnp
from jax import lax

BLK = 128
PIV = 512
KS = 8
NBP = 32
KU = 8
NU = 1024
N_LEAF = 4
N_FRONT = 8


def draw_front_entries(key, part):
    order = BLK * NBP
    split = KS * BLK
    horizontal = jax.random.uniform(jax.random.fold_in(key, 11), (order,), jnp.float32, 0.0, 1.0)
    vertical = jax.random.uniform(jax.random.fold_in(key, 12), (order,), jnp.float32, 0.0, 1.0)
    diagonal = jax.random.uniform(jax.random.fold_in(key, 13), (order,), jnp.float32, 5.0, 8.0)
    position = jnp.arange(order, dtype=jnp.int32)
    amplitude = 4.0 * 3.0 ** 0.5 / ((order - split) ** 0.5 + split ** 0.5)
    coupling = jax.random.uniform(jax.random.fold_in(key, 15), (order - split, split), jnp.float32, -amplitude, amplitude)
    left_part = jnp.concatenate([jnp.zeros((split, split), jnp.float32), coupling], axis=0)

    def one_block(inputs):
        block_horizontal, block_vertical, block_diagonal, block_position = inputs
        first_gap = block_horizontal[:, None] - horizontal[None, :]
        second_gap = block_vertical[:, None] - vertical[None, :]
        distance = jnp.sqrt(first_gap * first_gap + second_gap * second_gap)
        kernel = jnp.exp(-distance / 0.12)
        own_rows = jnp.take(left_part, block_position, axis=0)
        own_rows = jnp.concatenate([own_rows, jnp.zeros((block_position.shape[0], order - split), jnp.float32)], axis=1)
        mirrored = jnp.take(left_part, jnp.minimum(block_position, split - 1), axis=1).T
        mirrored = jnp.where(block_position[:, None] < split, mirrored, 0.0)
        kernel = kernel + own_rows + mirrored
        return jnp.where(block_position[:, None] == position[None, :], kernel + block_diagonal[:, None], kernel)
    row_blocks = lax.map(one_block, (horizontal.reshape(NBP, BLK), vertical.reshape(NBP, BLK), diagonal.reshape(NBP, BLK), position.reshape(NBP, BLK)))
    return row_blocks.reshape(NBP // N_LEAF, N_LEAF, BLK, NBP // N_FRONT, N_FRONT, BLK)


def draw_child_blocks(key, part):
    spread = 0.95 / NU ** 0.5
    noise = jax.random.uniform(jax.random.fold_in(key, 21), (N_LEAF, NU, NU), jnp.float32, -spread, spread)
    noise = (noise + jnp.swapaxes(noise, 1, 2)) * 0.5
    diagonal = jax.random.uniform(jax.random.fold_in(key, 22), (N_LEAF, NU), jnp.float32, 6.0, 9.0)
    index = jnp.arange(NU)
    same = index[:, None] == index[None, :]
    return jnp.where(same[None, :, :], diagonal[:, None, :], noise).astype(jnp.bfloat16)


def draw_child_map(key, part):
    cycles = jax.random.randint(jax.random.fold_in(key, 31), (N_LEAF, KU), 0, NBP // N_FRONT)
    cycles = cycles.at[0, 0].set(0)
    cycles = cycles.at[0, KU - 1].set(NBP // N_FRONT - 1)
    return (jnp.arange(KU, dtype=jnp.int32)[None, :] + N_FRONT * cycles).astype(jnp.int32)


def levels(stream_key, dims, cuts, low, high):
    factor_of, own = 1.0, jax.random.fold_in(stream_key, 6)
    for axis_at, shards_of in cuts:
        heights = jnp.exp(jax.random.uniform(jax.random.fold_in(own, axis_at), (shards_of,), jnp.float32, low / len(cuts), high / len(cuts)))
        factor_of = factor_of * jnp.repeat(heights, dims[axis_at] // shards_of).reshape([-1 if axis == axis_at else 1 for axis in range(len(dims))])
    return factor_of


def setup_inputs(seed: int = 0) -> dict:
    key_of = jax.random.split(jax.random.key(seed), 5)
    return {
        "front_entries": draw_front_entries(jax.random.fold_in(key_of[4], 71), 0),
        "child_panels": jnp.clip(jax.random.uniform(key_of[1], (N_LEAF, NU, PIV), jnp.float32, -0.053955078, 0.053955078) * levels(key_of[1], (N_LEAF, NU, PIV), ((0, 4), (1, 8)), -0.4, 0.0), -0.053955078, 0.053955078).astype(jnp.bfloat16),
        "child_blocks": draw_child_blocks(jax.random.fold_in(key_of[4], 71), 0),
        "child_map": draw_child_map(jax.random.fold_in(key_of[4], 71), 0),
    }


def reference(front_entries, child_panels, child_blocks, child_map):
    order = BLK * NBP
    assembled = front_entries.reshape(order, order)
    offsets = jnp.arange(BLK, dtype=jnp.int32)
    for child in range(N_LEAF):
        panel = child_panels[child]
        update = (child_blocks[child].astype(jnp.float32) - jnp.dot(panel.astype(jnp.float32), panel.T.astype(jnp.float32), preferred_element_type=jnp.float32)).astype(jnp.bfloat16)
        update = lax.optimization_barrier(update).astype(jnp.float32)
        places = (child_map[child][:, None] * BLK + offsets[None, :]).reshape(-1).astype(jnp.int32)
        assembled = assembled.at[places[:, None], places[None, :]].add(update)
    split = KS * BLK
    lower11 = jnp.linalg.cholesky(assembled[:split, :split])
    lower21 = lax.linalg.triangular_solve(lower11, assembled[split:, :split], left_side=False, lower=True, transpose_a=True)
    schur = assembled[split:, split:] - jnp.dot(lower21.astype(jnp.float32), lower21.T.astype(jnp.float32), precision=lax.Precision.HIGHEST, preferred_element_type=jnp.float32)
    result = jnp.zeros((order, order), jnp.float32)
    result = result.at[:split, :split].set(jnp.tril(lower11))
    result = result.at[split:, :split].set(lower21)
    result = result.at[split:, split:].set(schur)
    return result.reshape(NBP // N_LEAF, N_LEAF, BLK, NBP // N_FRONT, N_FRONT, BLK)
```

```python
import functools

import jax
import jax.numpy as jnp
from jax import lax
from jax.experimental import pallas as pl
from jax.experimental.pallas import tpu as pltpu
from jax.sharding import PartitionSpec as P

KS = 8
NT = (((1,), (1,)), ((), ()))
NN = (((1,), (0,)), ((), ()))
VMEM = pl.BlockSpec(memory_space=pltpu.VMEM)
SMEM = pl.BlockSpec(memory_space=pltpu.SMEM)
LIMIT = 56 * 1024 * 1024


def dot(a, b, dims):
    return lax.dot_general(a, b, dims, preferred_element_type=jnp.float32)


def halves(x):
    high = x.astype(jnp.bfloat16)
    return high, (x - high.astype(jnp.float32)).astype(jnp.bfloat16)


def dot3(a, b, dims):
    return dot(a[0], b[0], dims) + (dot(a[0], b[1], dims) + dot(a[1], b[0], dims))


def factor_block(a_ref, u_ref, z_ref):
    size = a_ref.shape[0]
    tiles = size // 8
    sub = lax.broadcasted_iota(jnp.int32, (8, size), 0)
    lane = lax.broadcasted_iota(jnp.int32, (8, size), 1)
    a = [a_ref[8 * t : 8 * t + 8, :] for t in range(tiles)]
    z = [jnp.where(lane == sub + 8 * t, 1.0, 0.0).astype(jnp.float32) for t in range(tiles)]

    def row(tile, s):
        return jnp.broadcast_to(tile[s : s + 1, :], (8, size))

    def column(tile, j):
        return jnp.broadcast_to(tile[:, j : j + 1], (8, size))

    for j in range(0, size, 2):
        t0, s = j // 8, j % 8
        r0, r1 = row(a[t0], s), row(a[t0], s + 1)
        q0, q1 = row(z[t0], s), row(z[t0], s + 1)
        p00, p01, p11 = column(r0, j), column(r0, j + 1), column(r1, j + 1)
        det = p00 * p11 - p01 * p01
        inv = pl.reciprocal(det, approx=True)
        inv = inv * (2.0 - det * inv)
        e0, e1 = (p11 * r0 - p01 * r1) * inv, (p00 * r1 - p01 * r0) * inv
        g0, g1 = (p11 * q0 - p01 * q1) * inv, (p00 * q1 - p01 * q0) * inv
        for t in range(t0, tiles):
            if t == t0 and s == 6:
                continue
            x, y = column(a[t], j), column(a[t], j + 1)
            if t == t0:
                x, y = jnp.where(sub > s + 1, x, 0.0), jnp.where(sub > s + 1, y, 0.0)
            a[t] = a[t] - (x * e0 + y * e1)
            z[t] = z[t] - (x * g0 + y * g1)
        d0 = lax.rsqrt(p00)
        ratio = p01 * d0 * d0
        d1 = lax.rsqrt(p11 - ratio * p01)
        u_ref[j : j + 1, :] = (r0 * d0)[:1]
        u_ref[j + 1 : j + 2, :] = ((r1 - ratio * r0) * d1)[:1]
        z_ref[j : j + 1, :] = (q0 * d0)[:1]
        z_ref[j + 1 : j + 2, :] = ((q1 - ratio * q0) * d1)[:1]


def cholesky_kernel(place, blocks_ref, l_ref, z_ref, a_ref, d_ref, u_ref):
    size = blocks_ref.shape[1]
    for j in range(KS):
        for i in range(j, KS):
            at = place(i, j)
            a_ref[i * size : (i + 1) * size, j * size : (j + 1) * size] = blocks_ref[
                at * size : (at + 1) * size, :
            ].astype(jnp.float32)
            if i > j:
                l_ref[j * size : (j + 1) * size, i * size : (i + 1) * size] = jnp.zeros(
                    (size, size), jnp.float32
                )
    d_ref[...] = a_ref[:size, :size]
    keep = lax.broadcasted_iota(jnp.int32, (size, size), 0) >= lax.broadcasted_iota(
        jnp.int32, (size, size), 1
    )

    def step(k, carry):
        z_now = z_ref.at[pl.ds(pl.multiple_of(k * size, size), size), :]
        factor_block(d_ref, u_ref, z_now)
        for now in range(KS):

            @pl.when(k == now)
            def _():
                low, high = now * size, (now + 1) * size
                l_ref[low:high, low:high] = jnp.where(keep, u_ref[...].T, 0.0)
                if now + 1 == KS:
                    return
                panel = dot3(halves(a_ref[high:, low:high]), halves(z_now[...]), NT)
                l_ref[high:, low:high] = panel
                parts = halves(panel)
                for j in range(now + 1, KS):
                    skip = (j - now - 1) * size
                    left = tuple(x[skip:] for x in parts)
                    right = tuple(x[skip : skip + size] for x in parts)
                    at = j * size
                    fresh = a_ref[at:, at : at + size] - dot3(left, right, NT)
                    if j == now + 1:
                        d_ref[...] = fresh[:size]
                    a_ref[at:, at : at + size] = fresh

        return carry

    lax.fori_loop(0, KS, step, 0)


def assemble_kernel(leaf_count, front_count, where_ref, map_ref, got_ref, front_ref, out_ref):
    children, spread, size, _ = got_ref.shape
    leaf_id, front_id = where_ref[0], where_ref[1]
    rows = out_ref.shape[1]
    for s in range(out_ref.shape[0]):
        out_ref[s] = front_ref[pl.ds(s, rows, stride=out_ref.shape[0]), :]
    for c in range(children):
        col = map_ref[c, front_id] // front_count
        for q in range(spread):
            at = pl.multiple_of(map_ref[c, leaf_id + leaf_count * q] // leaf_count * size, size)
            out_ref[col, pl.ds(at, size), :] += got_ref[c, q].astype(jnp.float32)


def solve_kernel(
    leaf_count, first, where_ref, l_ref, z_ref, rows_ref, tops_ref, full_ref, out_ref, s_ref, w_ref
):
    col_blocks, all_rows, size = full_ref.shape
    top = tops_ref.shape[0] // leaf_count // size
    rows = all_rows - top * size
    leaf_id, front_id = where_ref[0], where_ref[1]
    low = jnp.bfloat16
    for k in range(KS):
        at = slice(k * size, (k + 1) * size)
        inverse = z_ref[at, :].astype(low)
        own = rows_ref[k * rows : (k + 1) * rows, :]
        source = ((k % leaf_count) * top + k // leaf_count) * size
        met = tops_ref[source : source + size, first * size :]
        if k:
            before = l_ref[at, : k * size].astype(low)
            own = (own.astype(jnp.float32) - dot(s_ref[:, : k * size], before, NT)).astype(low)
            met = (met.astype(jnp.float32) - dot(before, w_ref[: k * size, :], NN)).astype(low)
        solved = dot(own, inverse, NT)
        s_ref[:, at] = solved.astype(low)
        w_ref[at, :] = dot(inverse, met, NN).astype(low)

        @pl.when(front_id == k)
        def _():
            out_ref[pl.ds(top * size * col_blocks, rows, stride=col_blocks), :] = solved
            for t in range(top):
                from_row = pl.multiple_of((t * leaf_count + leaf_id) * size, size)
                out_ref[pl.ds(t * size * col_blocks, size, stride=col_blocks), :] = l_ref[
                    pl.ds(from_row, size), at
                ]

    def complement(s):
        chunk = 256 if rows % 256 == 0 else size
        for r in range(0, rows, chunk):
            left = s_ref[r : r + chunk, :]
            right = w_ref[:, (s - first) * size : (s - first + 1) * size]
            begin = top * size + r
            out_ref[pl.ds(begin * col_blocks + s, chunk, stride=col_blocks), :] = full_ref[
                s, begin : begin + chunk, :
            ] - dot(left, right, NN)
        out_ref[pl.ds(s, top * size, stride=col_blocks), :] = jnp.zeros(
            (top * size, size), jnp.float32
        )

    for s in range(first, col_blocks):
        if s == 0:
            pl.when(front_id >= KS)(functools.partial(complement, s))
        else:
            complement(s)


def on_device(front_entries, child_panels, child_blocks, child_map):
    leaf_count = lax.axis_size("leaf")
    front_count = lax.axis_size("front")
    place = jnp.stack([lax.axis_index("leaf"), lax.axis_index("front")]).astype(jnp.int32)
    row_blocks, _, size, col_blocks, _, _ = front_entries.shape
    children = child_map.shape[0]
    spread = child_map.shape[1] // leaf_count
    rows = row_blocks * size
    top = KS // leaf_count
    first = KS // front_count
    params = pltpu.CompilerParams(vmem_limit_bytes=LIMIT)
    product = lax.dot_general(
        lax.all_gather(child_panels[0], "front", axis=0, tiled=True),
        child_panels[0],
        NT,
        preferred_element_type=jnp.float32,
    )
    update = (child_blocks[0].astype(jnp.float32) - product).astype(jnp.bfloat16)
    got = lax.all_to_all(
        update.reshape(spread, leaf_count, size, size), "leaf", split_axis=1, concat_axis=0
    )
    full = pl.pallas_call(
        functools.partial(assemble_kernel, leaf_count, front_count),
        out_shape=jax.ShapeDtypeStruct((col_blocks, rows, size), jnp.float32),
        in_specs=[SMEM, SMEM, VMEM, VMEM],
        out_specs=VMEM,
        compiler_params=params,
    )(
        place,
        child_map,
        got.reshape(children, spread, size, size),
        front_entries.reshape(rows * col_blocks, size),
    )
    tops = full[:, : top * size].astype(jnp.bfloat16)
    corner = lax.all_gather(tops[0], ("leaf", "front"), axis=0, tiled=True)
    below = lax.all_gather(full[0, top * size :].astype(jnp.bfloat16), "front", axis=0, tiled=True)
    across = jnp.swapaxes(tops, 0, 1).reshape(top * size, col_blocks * size)
    across = lax.all_gather(across, "leaf", axis=0, tiled=True)
    width = KS * size

    def corner_place(i, j):
        return ((i % leaf_count) * front_count + j) * top + i // leaf_count

    lower, inverses = pl.pallas_call(
        functools.partial(cholesky_kernel, corner_place),
        out_shape=[
            jax.ShapeDtypeStruct((width, width), jnp.float32),
            jax.ShapeDtypeStruct((width, size), jnp.float32),
        ],
        in_specs=[VMEM],
        out_specs=[VMEM, VMEM],
        scratch_shapes=[
            pltpu.VMEM((width, width), jnp.float32),
            pltpu.VMEM((size, size), jnp.float32),
            pltpu.VMEM((size, size), jnp.float32),
        ],
        compiler_params=params,
        cost_estimate=pl.CostEstimate(
            flops=8 * width**3, bytes_accessed=8 * width * width, transcendentals=0
        ),
    )(corner)
    result = pl.pallas_call(
        functools.partial(solve_kernel, leaf_count, first),
        out_shape=jax.ShapeDtypeStruct((rows * col_blocks, size), jnp.float32),
        in_specs=[SMEM] + [VMEM] * 5,
        out_specs=VMEM,
        scratch_shapes=[
            pltpu.VMEM((rows - top * size, width), jnp.bfloat16),
            pltpu.VMEM((width, (col_blocks - first) * size), jnp.bfloat16),
        ],
        compiler_params=params,
    )(place, lower, inverses, below, across, full)
    return result.reshape(row_blocks, 1, size, col_blocks, 1, size)


def solution(mesh):
    placed = (
        P(None, "leaf", None, None, "front", None),
        P("leaf", "front", None),
        P("leaf", None, "front"),
        P(),
    )
    return jax.shard_map(
        on_device,
        mesh=mesh,
        in_specs=placed,
        out_specs=P(None, "leaf", None, None, "front", None),
        check_vma=False,
    )
```

```python
import functools

import jax
import jax.numpy as jnp
from jax import lax
from jax.experimental import pallas as pl
from jax.experimental.pallas import tpu as pltpu
from jax.sharding import PartitionSpec as P

KS = 8
NT = (((1,), (1,)), ((), ()))
NN = (((1,), (0,)), ((), ()))
VMEM = pl.BlockSpec(memory_space=pltpu.VMEM)
SMEM = pl.BlockSpec(memory_space=pltpu.SMEM)
LIMIT = 56 * 1024 * 1024


def dot(a, b, dims):
    return lax.dot_general(a, b, dims, preferred_element_type=jnp.float32)


def halves(x):
    high = x.astype(jnp.bfloat16)
    return high, (x - high.astype(jnp.float32)).astype(jnp.bfloat16)


def dot3(a, b, dims):
    return dot(a[0], b[0], dims) + (dot(a[0], b[1], dims) + dot(a[1], b[0], dims))


def factor_block(a_ref, u_ref, z_ref):
    size = a_ref.shape[0]
    tiles = size // 8
    sub = lax.broadcasted_iota(jnp.int32, (8, size), 0)
    lane = lax.broadcasted_iota(jnp.int32, (8, size), 1)
    a = [a_ref[8 * t : 8 * t + 8, :] for t in range(tiles)]
    z = [jnp.where(lane == sub + 8 * t, 1.0, 0.0).astype(jnp.float32) for t in range(tiles)]

    def row(tile, s):
        return jnp.broadcast_to(tile[s : s + 1, :], (8, size))

    def column(tile, j):
        return jnp.broadcast_to(tile[:, j : j + 1], (8, size))

    for t0 in range(tiles):
        base = 8 * t0
        spread = [column(a[t0], base + k) for k in range(8)]
        e = {(m, k): row(spread[k], m) for k in range(8) for m in range(k + 1)}
        r = [row(a[t0], m) for m in range(8)]
        q = [row(z[t0], m) for m in range(8)]
        x = {t: [column(a[t], base + k) for k in range(8)] for t in range(t0 + 1, tiles)}
        w, v, solved = [None] * 8, [None] * 8, {}
        for j in range(0, 8, 2):
            p00, p01, p11 = e[j, j], e[j, j + 1], e[j + 1, j + 1]
            det = p00 * p11 - p01 * p01
            inv = pl.reciprocal(det, approx=True)
            inv = inv * (2.0 - det * inv)
            c00, c01, c11 = p00 * inv, p01 * inv, p11 * inv

            def pivot(first, second):
                return c11 * first - c01 * second, c00 * second - c01 * first

            for m in range(j + 2, 8):
                solved[j, m], solved[j + 1, m] = pivot(e[j, m], e[j + 1, m])
            for m in range(j + 2, 8):
                for k in range(m, 8):
                    e[m, k] = e[m, k] - (e[j, m] * solved[j, k] + e[j + 1, m] * solved[j + 1, k])
            w[j], w[j + 1] = pivot(r[j], r[j + 1])
            v[j], v[j + 1] = pivot(q[j], q[j + 1])
            for m in range(j + 2, 8):
                r[m] = r[m] - (e[j, m] * w[j] + e[j + 1, m] * w[j + 1])
                q[m] = q[m] - (e[j, m] * v[j] + e[j + 1, m] * v[j + 1])
            d0 = lax.rsqrt(p00)
            ratio = p01 * d0 * d0
            d1 = lax.rsqrt(p11 - ratio * p01)
            at = base + j
            u_ref[at : at + 1, :] = (r[j] * d0)[:1]
            u_ref[at + 1 : at + 2, :] = ((r[j + 1] - ratio * r[j]) * d1)[:1]
            z_ref[at : at + 1, :] = (q[j] * d0)[:1]
            z_ref[at + 1 : at + 2, :] = ((q[j + 1] - ratio * q[j]) * d1)[:1]
        if t0 + 1 == tiles:
            break
        for j in (4, 2, 0):
            for i in (j, j + 1):
                for k in range(j + 2, 8):
                    w[i] = w[i] - solved[i, k] * w[k]
                    v[i] = v[i] - solved[i, k] * v[k]
        for t in range(t0 + 1, tiles):
            y = x[t]
            terms = [y[k] * w[k] for k in range(8)]
            a[t] = a[t] - (
                ((terms[0] + terms[1]) + (terms[2] + terms[3]))
                + ((terms[4] + terms[5]) + (terms[6] + terms[7]))
            )
            terms = [y[k] * v[k] for k in range(8)]
            z[t] = z[t] - (
                ((terms[0] + terms[1]) + (terms[2] + terms[3]))
                + ((terms[4] + terms[5]) + (terms[6] + terms[7]))
            )


def cholesky_kernel(place, blocks_ref, l_ref, z_ref, a_ref, d_ref, u_ref):
    size = blocks_ref.shape[1]
    for j in range(KS):
        for i in range(j, KS):
            at = place(i, j)
            a_ref[i * size : (i + 1) * size, j * size : (j + 1) * size] = blocks_ref[
                at * size : (at + 1) * size, :
            ].astype(jnp.float32)
            if i > j:
                l_ref[j * size : (j + 1) * size, i * size : (i + 1) * size] = jnp.zeros(
                    (size, size), jnp.float32
                )
    d_ref[...] = a_ref[:size, :size]
    keep = lax.broadcasted_iota(jnp.int32, (size, size), 0) >= lax.broadcasted_iota(
        jnp.int32, (size, size), 1
    )

    def step(k, carry):
        z_now = z_ref.at[pl.ds(pl.multiple_of(k * size, size), size), :]
        factor_block(d_ref, u_ref, z_now)
        for now in range(KS):

            @pl.when(k == now)
            def _():
                low, high = now * size, (now + 1) * size
                l_ref[low:high, low:high] = jnp.where(keep, u_ref[...].T, 0.0)
                if now + 1 == KS:
                    return
                panel = dot3(halves(a_ref[high:, low:high]), halves(z_now[...]), NT)
                l_ref[high:, low:high] = panel
                parts = halves(panel)
                for j in range(now + 1, KS):
                    skip = (j - now - 1) * size
                    left = tuple(x[skip:] for x in parts)
                    right = tuple(x[skip : skip + size] for x in parts)
                    at = j * size
                    fresh = a_ref[at:, at : at + size] - dot3(left, right, NT)
                    if j == now + 1:
                        d_ref[...] = fresh[:size]
                    a_ref[at:, at : at + size] = fresh

        return carry

    lax.fori_loop(0, KS, step, 0)


def assemble_kernel(leaf_count, front_count, where_ref, map_ref, got_ref, front_ref, out_ref):
    children, spread, size, _ = got_ref.shape
    leaf_id, front_id = where_ref[0], where_ref[1]
    rows = out_ref.shape[1]
    for s in range(out_ref.shape[0]):
        out_ref[s] = front_ref[pl.ds(s, rows, stride=out_ref.shape[0]), :]
    for c in range(children):
        col = map_ref[c, front_id] // front_count
        for q in range(spread):
            at = pl.multiple_of(map_ref[c, leaf_id + leaf_count * q] // leaf_count * size, size)
            out_ref[col, pl.ds(at, size), :] += got_ref[c, q].astype(jnp.float32)


def solve_kernel(
    leaf_count, front_count, first, where_ref, l_ref, z_ref, rows_ref, tops_ref, full_ref, out_ref, s_ref, w_ref
):
    col_blocks, all_rows, size = full_ref.shape
    top = tops_ref.shape[0] // leaf_count // size
    rows = all_rows - top * size
    leaf_id, front_id = where_ref[0], where_ref[1]
    low = jnp.bfloat16
    for k in range(KS):
        at = slice(k * size, (k + 1) * size)
        inverse = z_ref[at, :].astype(low)
        distance = lax.rem(front_id - k + front_count, front_count)
        own = rows_ref[pl.ds(pl.multiple_of(distance * rows, size), rows), :]
        distance = lax.rem(leaf_id - k % leaf_count + leaf_count, leaf_count)
        source = (distance * top + k // leaf_count) * size
        met = tops_ref[pl.ds(pl.multiple_of(source, size), size), first * size :]
        if k:
            before = l_ref[at, : k * size].astype(low)
            own = (own.astype(jnp.float32) - dot(s_ref[:, : k * size], before, NT)).astype(low)
            met = (met.astype(jnp.float32) - dot(before, w_ref[: k * size, :], NN)).astype(low)
        solved = dot(own, inverse, NT)
        s_ref[:, at] = solved.astype(low)
        w_ref[at, :] = dot(inverse, met, NN).astype(low)

        @pl.when(front_id == k)
        def _():
            out_ref[pl.ds(top * size * col_blocks, rows, stride=col_blocks), :] = solved
            for t in range(top):
                from_row = pl.multiple_of((t * leaf_count + leaf_id) * size, size)
                out_ref[pl.ds(t * size * col_blocks, size, stride=col_blocks), :] = l_ref[
                    pl.ds(from_row, size), at
                ]

    def complement(s):
        chunk = 256 if rows % 256 == 0 else size
        for r in range(0, rows, chunk):
            left = s_ref[r : r + chunk, :]
            right = w_ref[:, (s - first) * size : (s - first + 1) * size]
            begin = top * size + r
            out_ref[pl.ds(begin * col_blocks + s, chunk, stride=col_blocks), :] = full_ref[
                s, begin : begin + chunk, :
            ] - dot(left, right, NN)
        out_ref[pl.ds(s, top * size, stride=col_blocks), :] = jnp.zeros(
            (top * size, size), jnp.float32
        )

    for s in range(first, col_blocks):
        if s == 0:
            pl.when(front_id >= KS)(functools.partial(complement, s))
        else:
            complement(s)


def gather_by_distance(x, axis):
    count = lax.axis_size(axis)
    pieces = [x]
    for d in range(1, count):
        pieces.append(lax.ppermute(x, axis, [(i, (i + d) % count) for i in range(count)]))
    return jnp.concatenate(pieces, axis=0)


def on_device(front_entries, child_panels, child_blocks, child_map):
    leaf_count = lax.axis_size("leaf")
    front_count = lax.axis_size("front")
    place = jnp.stack([lax.axis_index("leaf"), lax.axis_index("front")]).astype(jnp.int32)
    row_blocks, _, size, col_blocks, _, _ = front_entries.shape
    children = child_map.shape[0]
    spread = child_map.shape[1] // leaf_count
    rows = row_blocks * size
    top = KS // leaf_count
    first = KS // front_count
    params = pltpu.CompilerParams(vmem_limit_bytes=LIMIT)
    product = lax.dot_general(
        lax.all_gather(child_panels[0], "front", axis=0, tiled=True),
        child_panels[0],
        NT,
        preferred_element_type=jnp.float32,
    )
    update = (child_blocks[0].astype(jnp.float32) - product).astype(jnp.bfloat16)
    got = lax.all_to_all(
        update.reshape(spread, leaf_count, size, size), "leaf", split_axis=1, concat_axis=0
    )
    full = pl.pallas_call(
        functools.partial(assemble_kernel, leaf_count, front_count),
        out_shape=jax.ShapeDtypeStruct((col_blocks, rows, size), jnp.float32),
        in_specs=[SMEM, SMEM, VMEM, VMEM],
        out_specs=VMEM,
        compiler_params=params,
    )(
        place,
        child_map,
        got.reshape(children, spread, size, size),
        front_entries.reshape(rows * col_blocks, size),
    )
    tops = full[:, : top * size].astype(jnp.bfloat16)
    corner = lax.all_gather(tops[0], ("leaf", "front"), axis=0, tiled=True)
    below = gather_by_distance(full[0, top * size :].astype(jnp.bfloat16), "front")
    across = jnp.swapaxes(tops, 0, 1).reshape(top * size, col_blocks * size)
    across = gather_by_distance(across, "leaf")
    width = KS * size

    def corner_place(i, j):
        return ((i % leaf_count) * front_count + j) * top + i // leaf_count

    lower, inverses = pl.pallas_call(
        functools.partial(cholesky_kernel, corner_place),
        out_shape=[
            jax.ShapeDtypeStruct((width, width), jnp.float32),
            jax.ShapeDtypeStruct((width, size), jnp.float32),
        ],
        in_specs=[VMEM],
        out_specs=[VMEM, VMEM],
        scratch_shapes=[
            pltpu.VMEM((width, width), jnp.float32),
            pltpu.VMEM((size, size), jnp.float32),
            pltpu.VMEM((size, size), jnp.float32),
        ],
        compiler_params=params,
        cost_estimate=pl.CostEstimate(
            flops=8 * width**3, bytes_accessed=8 * width * width, transcendentals=0
        ),
    )(corner)
    result = pl.pallas_call(
        functools.partial(solve_kernel, leaf_count, front_count, first),
        out_shape=jax.ShapeDtypeStruct((rows * col_blocks, size), jnp.float32),
        in_specs=[SMEM] + [VMEM] * 5,
        out_specs=VMEM,
        scratch_shapes=[
            pltpu.VMEM((rows - top * size, width), jnp.bfloat16),
            pltpu.VMEM((width, (col_blocks - first) * size), jnp.bfloat16),
        ],
        compiler_params=params,
    )(place, lower, inverses, below, across, full)
    return result.reshape(row_blocks, 1, size, col_blocks, 1, size)


def solution(mesh):
    placed = (
        P(None, "leaf", None, None, "front", None),
        P("leaf", "front", None),
        P("leaf", None, "front"),
        P(),
    )
    return jax.shard_map(
        on_device,
        mesh=mesh,
        in_specs=placed,
        out_specs=P(None, "leaf", None, None, "front", None),
        check_vma=False,
    )
```

```python
import functools

import jax
import jax.numpy as jnp
from jax import lax
from jax.experimental import pallas as pl
from jax.experimental.pallas import tpu as pltpu
from jax.sharding import PartitionSpec as P

KS = 8
NT = (((1,), (1,)), ((), ()))
NN = (((1,), (0,)), ((), ()))
VMEM = pl.BlockSpec(memory_space=pltpu.VMEM)
SMEM = pl.BlockSpec(memory_space=pltpu.SMEM)
LIMIT = 56 * 1024 * 1024


def dot(a, b, dims):
    return lax.dot_general(a, b, dims, preferred_element_type=jnp.float32)


def halves(x):
    high = x.astype(jnp.bfloat16)
    return high, (x - high.astype(jnp.float32)).astype(jnp.bfloat16)


def dot3(a, b, dims):
    return dot(a[0], b[0], dims) + (dot(a[0], b[1], dims) + dot(a[1], b[0], dims))


def factor_block(a_ref, u_ref, z_ref):
    size = a_ref.shape[0]
    tiles = size // 8
    sub = lax.broadcasted_iota(jnp.int32, (8, size), 0)
    lane = lax.broadcasted_iota(jnp.int32, (8, size), 1)
    a = [a_ref[8 * t : 8 * t + 8, :] for t in range(tiles)]
    z = [jnp.where(lane == sub + 8 * t, 1.0, 0.0).astype(jnp.float32) for t in range(tiles)]

    def row(tile, s):
        return jnp.broadcast_to(tile[s : s + 1, :], (8, size))

    def column(tile, j):
        return jnp.broadcast_to(tile[:, j : j + 1], (8, size))

    for t0 in range(tiles):
        base = 8 * t0
        spread = [column(a[t0], base + k) for k in range(8)]
        e = {(m, k): row(spread[k], m) for k in range(8) for m in range(k + 1)}
        r = [row(a[t0], m) for m in range(8)]
        q = [row(z[t0], m) for m in range(8)]
        x = {t: [column(a[t], base + k) for k in range(8)] for t in range(t0 + 1, tiles)}
        w, v, solved = [None] * 8, [None] * 8, {}
        for j in range(0, 8, 2):
            p00, p01, p11 = e[j, j], e[j, j + 1], e[j + 1, j + 1]
            det = p00 * p11 - p01 * p01
            inv = pl.reciprocal(det, approx=True)
            inv = inv * (2.0 - det * inv)
            c00, c01, c11 = p00 * inv, p01 * inv, p11 * inv

            def pivot(first, second):
                return c11 * first - c01 * second, c00 * second - c01 * first

            for m in range(j + 2, 8):
                solved[j, m], solved[j + 1, m] = pivot(e[j, m], e[j + 1, m])
            for m in range(j + 2, 8):
                for k in range(m, 8):
                    e[m, k] = e[m, k] - (e[j, m] * solved[j, k] + e[j + 1, m] * solved[j + 1, k])
            w[j], w[j + 1] = pivot(r[j], r[j + 1])
            v[j], v[j + 1] = pivot(q[j], q[j + 1])
            for m in range(j + 2, 8):
                r[m] = r[m] - (e[j, m] * w[j] + e[j + 1, m] * w[j + 1])
                q[m] = q[m] - (e[j, m] * v[j] + e[j + 1, m] * v[j + 1])
            d0 = lax.rsqrt(p00)
            ratio = p01 * d0 * d0
            d1 = lax.rsqrt(p11 - ratio * p01)
            at = base + j
            u_ref[at : at + 1, :] = (r[j] * d0)[:1]
            u_ref[at + 1 : at + 2, :] = ((r[j + 1] - ratio * r[j]) * d1)[:1]
            z_ref[at : at + 1, :] = (q[j] * d0)[:1]
            z_ref[at + 1 : at + 2, :] = ((q[j + 1] - ratio * q[j]) * d1)[:1]
        if t0 + 1 == tiles:
            break
        for j in (4, 2, 0):
            for i in (j, j + 1):
                for k in range(j + 2, 8):
                    w[i] = w[i] - solved[i, k] * w[k]
                    v[i] = v[i] - solved[i, k] * v[k]
        for t in range(t0 + 1, tiles):
            y = x[t]
            terms = [y[k] * w[k] for k in range(8)]
            a[t] = a[t] - (
                ((terms[0] + terms[1]) + (terms[2] + terms[3]))
                + ((terms[4] + terms[5]) + (terms[6] + terms[7]))
            )
            terms = [y[k] * v[k] for k in range(8)]
            z[t] = z[t] - (
                ((terms[0] + terms[1]) + (terms[2] + terms[3]))
                + ((terms[4] + terms[5]) + (terms[6] + terms[7]))
            )


def cholesky_kernel(place, blocks_ref, l_ref, z_ref, a_ref, d_ref, u_ref):
    size = blocks_ref.shape[1]
    for j in range(KS):
        for i in range(j, KS):
            at = place(i, j)
            a_ref[i * size : (i + 1) * size, j * size : (j + 1) * size] = blocks_ref[
                at * size : (at + 1) * size, :
            ].astype(jnp.float32)
            if i > j:
                l_ref[j * size : (j + 1) * size, i * size : (i + 1) * size] = jnp.zeros(
                    (size, size), jnp.float32
                )
    d_ref[...] = a_ref[:size, :size]
    keep = lax.broadcasted_iota(jnp.int32, (size, size), 0) >= lax.broadcasted_iota(
        jnp.int32, (size, size), 1
    )

    def step(k, carry):
        z_now = z_ref.at[pl.ds(pl.multiple_of(k * size, size), size), :]
        factor_block(d_ref, u_ref, z_now)
        for now in range(KS):

            @pl.when(k == now)
            def _():
                low, high = now * size, (now + 1) * size
                l_ref[low:high, low:high] = jnp.where(keep, u_ref[...].T, 0.0)
                if now + 1 == KS:
                    return
                panel = dot3(halves(a_ref[high:, low:high]), halves(z_now[...]), NT)
                l_ref[high:, low:high] = panel
                parts = halves(panel)
                for j in range(now + 1, KS):
                    skip = (j - now - 1) * size
                    left = tuple(x[skip:] for x in parts)
                    right = tuple(x[skip : skip + size] for x in parts)
                    at = j * size
                    fresh = a_ref[at:, at : at + size] - dot3(left, right, NT)
                    if j == now + 1:
                        d_ref[...] = fresh[:size]
                    a_ref[at:, at : at + size] = fresh

        return carry

    lax.fori_loop(0, KS, step, 0)


def assemble_kernel(leaf_count, front_count, where_ref, map_ref, got_ref, front_ref, out_ref):
    children, spread, size, _ = got_ref.shape
    leaf_id, front_id = where_ref[0], where_ref[1]
    rows = out_ref.shape[1]
    for s in range(out_ref.shape[0]):
        out_ref[s] = front_ref[pl.ds(s, rows, stride=out_ref.shape[0]), :]
    for c in range(children):
        col = map_ref[c, front_id] // front_count
        for q in range(spread):
            at = pl.multiple_of(map_ref[c, leaf_id + leaf_count * q] // leaf_count * size, size)
            out_ref[col, pl.ds(at, size), :] += got_ref[c, q].astype(jnp.float32)


def solve_kernel(
    leaf_count, first, where_ref, l_ref, z_ref, rows_ref, tops_ref, full_ref, out_ref, s_ref, w_ref
):
    col_blocks, all_rows, size = full_ref.shape
    top = tops_ref.shape[0] // leaf_count // size
    rows = all_rows - top * size
    leaf_id, front_id = where_ref[0], where_ref[1]
    low = jnp.bfloat16
    for k in range(KS):
        at = slice(k * size, (k + 1) * size)
        inverse = z_ref[at, :].astype(low)
        own = rows_ref[k * rows : (k + 1) * rows, :]
        distance = lax.rem(leaf_id - k % leaf_count + leaf_count, leaf_count)
        source = (distance * top + k // leaf_count) * size
        met = tops_ref[pl.ds(pl.multiple_of(source, size), size), first * size :]
        if k:
            before = l_ref[at, : k * size].astype(low)
            own = (own.astype(jnp.float32) - dot(s_ref[:, : k * size], before, NT)).astype(low)
            met = (met.astype(jnp.float32) - dot(before, w_ref[: k * size, :], NN)).astype(low)
        solved = dot(own, inverse, NT)
        s_ref[:, at] = solved.astype(low)
        w_ref[at, :] = dot(inverse, met, NN).astype(low)

        @pl.when(front_id == k)
        def _():
            out_ref[pl.ds(top * size * col_blocks, rows, stride=col_blocks), :] = solved
            for t in range(top):
                from_row = pl.multiple_of((t * leaf_count + leaf_id) * size, size)
                out_ref[pl.ds(t * size * col_blocks, size, stride=col_blocks), :] = l_ref[
                    pl.ds(from_row, size), at
                ]

    def complement(s):
        chunk = 256 if rows % 256 == 0 else size
        for r in range(0, rows, chunk):
            left = s_ref[r : r + chunk, :]
            right = w_ref[:, (s - first) * size : (s - first + 1) * size]
            begin = top * size + r
            out_ref[pl.ds(begin * col_blocks + s, chunk, stride=col_blocks), :] = full_ref[
                s, begin : begin + chunk, :
            ] - dot(left, right, NN)
        out_ref[pl.ds(s, top * size, stride=col_blocks), :] = jnp.zeros(
            (top * size, size), jnp.float32
        )

    for s in range(first, col_blocks):
        if s == 0:
            pl.when(front_id >= KS)(functools.partial(complement, s))
        else:
            complement(s)


MESH = pl.DeviceIdType.MESH
DMA = pltpu.SemaphoreType.DMA


def ring_position(member, count):
    side = lax.rem(member, 2)
    step = lax.div(member, 2)
    return step + side * (count - 1 - 2 * step)


def ring_member(position, count):
    side = lax.div(position, count // 2)
    return 2 * (position + side * (count - 1 - 2 * position)) + side


def behind(position, steps, count):
    return lax.rem(position - steps + count, count)


def ring_hops(position, count, first, slot, sems):
    send, recv = sems
    half = count // 2
    rows = first.shape[0]
    after = ring_member(lax.rem(position + 1, count), count)
    ahead = ring_member(behind(position, 1, count), count)

    def hop(way, s):
        to = s if way == 0 else count - s
        source = first if s == 1 else slot(to - 1 if way == 0 else to + 1)
        target = slot(to)
        if s == half:
            part = pl.ds(0, rows // 2) if way == 0 else pl.ds(rows // 2, rows // 2)
            source, target = source.at[part], target.at[part]
        return pltpu.make_async_remote_copy(
            src_ref=source,
            dst_ref=target,
            send_sem=send.at[way, s],
            recv_sem=recv.at[way, s],
            device_id={"front": after if way == 0 else ahead},
            device_id_type=MESH,
        )

    return hop, (after, ahead)


def ring_run(hop, half, ready):
    for way in (0, 1):
        hop(way, 1).start()
    ready(0)
    for s in range(1, half + 1):
        for way in (0, 1):
            hop(way, s).wait_recv()
            if s < half:
                hop(way, s + 1).start()
        ready(s)
        if s < half:
            ready(2 * half - s)


def ring_end(hop, half):
    for s in range(1, half + 1):
        for way in (0, 1):
            hop(way, s).wait_send()


def greet(barrier, devices):
    for device in devices:
        pl.semaphore_signal(barrier, inc=1, device_id=device, device_id_type=MESH)
    pl.semaphore_wait(barrier, len(devices))


def update_kernel(
    leaf_count, front_count, panel_ref, blocks_ref, got_ref,
    slots, stage, land, ring_send, ring_recv, out_send, out_recv,
):
    leaf_id, front_id = lax.axis_index("leaf"), lax.axis_index("front")
    size = panel_ref.shape[0]
    half = front_count // 2
    position = ring_position(front_id, front_count)
    hop, beside = ring_hops(
        position, front_count, panel_ref, lambda s: slots.at[s], (ring_send, ring_recv)
    )
    greet(
        pltpu.get_barrier_semaphore(),
        [{"front": f} for f in beside]
        + [{"leaf": lax.rem(leaf_id + d, leaf_count)} for d in range(1, leaf_count)],
    )

    def deliver(s):
        block = ring_member(behind(position, s, front_count), front_count)
        owner, turn = lax.rem(block, leaf_count), lax.div(block, leaf_count)
        copy = pltpu.make_async_remote_copy(
            src_ref=stage.at[s],
            dst_ref=land.at[leaf_id, turn],
            send_sem=out_send.at[s],
            recv_sem=out_recv.at[leaf_id, turn],
            device_id={"leaf": owner},
            device_id_type=MESH,
        )
        return block, owner, turn, copy

    def ready(s):
        block, owner, turn, copy = deliver(s)
        rows = panel_ref[...] if s == 0 else slots[s]
        given = blocks_ref[pl.ds(pl.multiple_of(block * size, size), size), :]
        product = dot(rows, panel_ref[...], NT)
        value = (given.astype(jnp.float32) - product).astype(jnp.bfloat16)
        stage[s] = value

        @pl.when(owner == leaf_id)
        def _():
            land[leaf_id, turn] = value

        @pl.when(owner != leaf_id)
        def _():
            copy.start()

    ring_run(hop, half, ready)
    for d in range(1, leaf_count):
        source = lax.rem(leaf_id + d, leaf_count)
        for turn in range(land.shape[1]):
            pltpu.make_async_remote_copy(
                src_ref=stage.at[0],
                dst_ref=land.at[source, turn],
                send_sem=out_send.at[0],
                recv_sem=out_recv.at[source, turn],
                device_id={"leaf": source},
                device_id_type=MESH,
            ).wait_recv()
    got_ref[...] = land[...]
    for s in range(front_count):
        _, owner, _, copy = deliver(s)
        pl.when(owner != leaf_id)(copy.wait_send)
    ring_end(hop, half)


def corner_kernel(
    leaf_count, front_count, piece_ref, out_ref,
    held, ring_send, ring_recv, far_send, far_recv, near_send, near_recv,
):
    leaf_id, front_id = lax.axis_index("leaf"), lax.axis_index("front")
    rows = piece_ref.shape[0]
    half = front_count // 2
    chips = leaf_count // 2
    chip, core = lax.div(leaf_id, 2), lax.rem(leaf_id, 2)
    mate = leaf_id + 1 - 2 * core
    position = ring_position(front_id, front_count)
    hop, beside = ring_hops(
        position,
        front_count,
        piece_ref,
        lambda s: held.at[leaf_id, s],
        (ring_send, ring_recv),
    )
    greet(
        pltpu.get_barrier_semaphore(),
        [{"front": f} for f in beside]
        + [{"leaf": 2 * lax.rem(chip + d, chips) + core} for d in range(1, chips)]
        + [{"leaf": mate}],
    )

    def far(d, s, source):
        return pltpu.make_async_remote_copy(
            src_ref=held.at[source, s],
            dst_ref=held.at[source, s],
            send_sem=far_send.at[d - 1, s],
            recv_sem=far_recv.at[d - 1, s],
            device_id={"leaf": 2 * lax.rem(chip + d, chips) + core},
            device_id_type=MESH,
        )

    def near(d, s, source):
        return pltpu.make_async_remote_copy(
            src_ref=held.at[source, s],
            dst_ref=held.at[source, s],
            send_sem=near_send.at[d, s],
            recv_sem=near_recv.at[d, s],
            device_id={"leaf": mate},
            device_id_type=MESH,
        )

    held[leaf_id, 0] = piece_ref[...]

    def ready(s):
        for d in range(1, chips):
            far(d, s, leaf_id).start()
        near(0, s, leaf_id).start()

    ring_run(hop, half, ready)
    order = [0] + [t for s in range(1, half) for t in (s, front_count - s)] + [half]
    for s in order:
        for d in range(1, chips):
            source = 2 * behind(chip, d, chips) + core
            far(d, s, source).wait_recv()
            near(d, s, source).start()
    for s in order:
        for d in range(chips):
            near(d, s, 2 * behind(chip, d, chips) + 1 - core).wait_recv()
    for s in range(front_count):
        column = ring_member(behind(position, s, front_count), front_count)
        for source in range(leaf_count):
            at = pl.multiple_of((source * front_count + column) * rows, rows)
            out_ref[pl.ds(at, rows), :] = held[source, s]
    for s in range(front_count):
        for d in range(1, chips):
            far(d, s, leaf_id).wait_send()
        for d in range(chips):
            near(d, s, leaf_id).wait_send()
    ring_end(hop, half)


def gather_by_distance(x, axis):
    count = lax.axis_size(axis)
    pieces = [x]
    for d in range(1, count):
        pieces.append(lax.ppermute(x, axis, [(i, (i + d) % count) for i in range(count)]))
    return jnp.concatenate(pieces, axis=0)


def on_device(front_entries, child_panels, child_blocks, child_map):
    leaf_count = lax.axis_size("leaf")
    front_count = lax.axis_size("front")
    place = jnp.stack([lax.axis_index("leaf"), lax.axis_index("front")]).astype(jnp.int32)
    row_blocks, _, size, col_blocks, _, _ = front_entries.shape
    children = child_map.shape[0]
    spread = child_map.shape[1] // leaf_count
    rows = row_blocks * size
    top = KS // leaf_count
    first = KS // front_count
    params = pltpu.CompilerParams(vmem_limit_bytes=LIMIT)
    piv = child_panels.shape[2]
    half = front_count // 2
    ring = [DMA((2, half + 1)), DMA((2, half + 1))]
    got = pl.pallas_call(
        functools.partial(update_kernel, leaf_count, front_count),
        out_shape=jax.ShapeDtypeStruct((children, spread, size, size), jnp.bfloat16),
        in_specs=[VMEM, VMEM],
        out_specs=VMEM,
        scratch_shapes=[
            pltpu.VMEM((front_count, size, piv), jnp.bfloat16),
            pltpu.VMEM((front_count, size, size), jnp.bfloat16),
            pltpu.VMEM((children, spread, size, size), jnp.bfloat16),
        ]
        + ring
        + [DMA((front_count,)), DMA((children, spread))],
        compiler_params=pltpu.CompilerParams(
            vmem_limit_bytes=LIMIT, collective_id=0, has_side_effects=True
        ),
    )(child_panels[0], child_blocks[0])
    full = pl.pallas_call(
        functools.partial(assemble_kernel, leaf_count, front_count),
        out_shape=jax.ShapeDtypeStruct((col_blocks, rows, size), jnp.float32),
        in_specs=[SMEM, SMEM, VMEM, VMEM],
        out_specs=VMEM,
        compiler_params=params,
    )(
        place,
        child_map,
        got,
        front_entries.reshape(rows * col_blocks, size),
    )
    tops = full[:, : top * size].astype(jnp.bfloat16)
    chips = leaf_count // 2
    corner = pl.pallas_call(
        functools.partial(corner_kernel, leaf_count, front_count),
        out_shape=jax.ShapeDtypeStruct(
            (leaf_count * front_count * top * size, size), jnp.bfloat16
        ),
        in_specs=[VMEM],
        out_specs=VMEM,
        scratch_shapes=[pltpu.VMEM((leaf_count, front_count, top * size, size), jnp.bfloat16)]
        + ring
        + [DMA((max(chips - 1, 1), front_count))] * 2
        + [DMA((chips, front_count))] * 2,
        compiler_params=pltpu.CompilerParams(
            vmem_limit_bytes=LIMIT, collective_id=1, has_side_effects=True
        ),
    )(tops[0])
    below = full[0, top * size :].astype(jnp.bfloat16)
    across = jnp.swapaxes(tops, 0, 1).reshape(top * size, col_blocks * size)
    corner, below, across = lax.optimization_barrier((corner, below, across))
    below = lax.all_gather(below, "front", axis=0, tiled=True)
    across = gather_by_distance(across, "leaf")
    width = KS * size

    def corner_place(i, j):
        return ((i % leaf_count) * front_count + j) * top + i // leaf_count

    lower, inverses = pl.pallas_call(
        functools.partial(cholesky_kernel, corner_place),
        out_shape=[
            jax.ShapeDtypeStruct((width, width), jnp.float32),
            jax.ShapeDtypeStruct((width, size), jnp.float32),
        ],
        in_specs=[VMEM],
        out_specs=[VMEM, VMEM],
        scratch_shapes=[
            pltpu.VMEM((width, width), jnp.float32),
            pltpu.VMEM((size, size), jnp.float32),
            pltpu.VMEM((size, size), jnp.float32),
        ],
        compiler_params=params,
        cost_estimate=pl.CostEstimate(
            flops=8 * width**3, bytes_accessed=8 * width * width, transcendentals=0
        ),
    )(corner)
    result = pl.pallas_call(
        functools.partial(solve_kernel, leaf_count, first),
        out_shape=jax.ShapeDtypeStruct((rows * col_blocks, size), jnp.float32),
        in_specs=[SMEM] + [VMEM] * 5,
        out_specs=VMEM,
        scratch_shapes=[
            pltpu.VMEM((rows - top * size, width), jnp.bfloat16),
            pltpu.VMEM((width, (col_blocks - first) * size), jnp.bfloat16),
        ],
        compiler_params=params,
    )(place, lower, inverses, below, across, full)
    return result.reshape(row_blocks, 1, size, col_blocks, 1, size)


def solution(mesh):
    placed = (
        P(None, "leaf", None, None, "front", None),
        P("leaf", "front", None),
        P("leaf", None, "front"),
        P(),
    )
    return jax.shard_map(
        on_device,
        mesh=mesh,
        in_specs=placed,
        out_specs=P(None, "leaf", None, None, "front", None),
        check_vma=False,
    )
```

```python
import functools

import jax
import jax.numpy as jnp
from jax import lax
from jax.experimental import pallas as pl
from jax.experimental.pallas import tpu as pltpu
from jax.sharding import PartitionSpec as P

KS = 8
NT = (((1,), (1,)), ((), ()))
NN = (((1,), (0,)), ((), ()))
VMEM = pl.BlockSpec(memory_space=pltpu.VMEM)
SMEM = pl.BlockSpec(memory_space=pltpu.SMEM)
LIMIT = 56 * 1024 * 1024


def dot(a, b, dims):
    return lax.dot_general(a, b, dims, preferred_element_type=jnp.float32)


def halves(x):
    high = x.astype(jnp.bfloat16)
    return high, (x - high.astype(jnp.float32)).astype(jnp.bfloat16)


def dot3(a, b, dims):
    return dot(a[0], b[0], dims) + (dot(a[0], b[1], dims) + dot(a[1], b[0], dims))


def factor_half(a_ref, u_ref):
    size, width = a_ref.shape
    tiles = size // 8
    sub = lax.broadcasted_iota(jnp.int32, (8, width), 0)
    lane = lax.broadcasted_iota(jnp.int32, (8, width), 1)
    a = [
        jnp.where(
            lane < size,
            a_ref[8 * t : 8 * t + 8, :],
            jnp.where(lane == sub + (size + 8 * t), 1.0, 0.0),
        )
        for t in range(tiles)
    ]

    def row(tile, s):
        return jnp.broadcast_to(tile[s : s + 1, :], (8, width))

    def column(tile, j):
        return jnp.broadcast_to(tile[:, j : j + 1], (8, width))

    for t0 in range(tiles):
        base = 8 * t0
        spread = [column(a[t0], base + k) for k in range(8)]
        e = {(m, k): row(spread[k], m) for k in range(8) for m in range(k + 1)}
        r = [row(a[t0], m) for m in range(8)]
        x = {t: [column(a[t], base + k) for k in range(8)] for t in range(t0 + 1, tiles)}
        w, solved = [None] * 8, {}
        for j in range(0, 8, 2):
            p00, p01, p11 = e[j, j], e[j, j + 1], e[j + 1, j + 1]
            det = p00 * p11 - p01 * p01
            inv = pl.reciprocal(det, approx=True)
            inv = inv * (2.0 - det * inv)
            c00, c01, c11 = p00 * inv, p01 * inv, p11 * inv

            def pivot(first, second):
                return c11 * first - c01 * second, c00 * second - c01 * first

            for m in range(j + 2, 8):
                solved[j, m], solved[j + 1, m] = pivot(e[j, m], e[j + 1, m])
            for m in range(j + 2, 8):
                for k in range(m, 8):
                    e[m, k] = e[m, k] - (e[j, m] * solved[j, k] + e[j + 1, m] * solved[j + 1, k])
            w[j], w[j + 1] = pivot(r[j], r[j + 1])
            for m in range(j + 2, 8):
                r[m] = r[m] - (e[j, m] * w[j] + e[j + 1, m] * w[j + 1])
            d0 = lax.rsqrt(p00)
            ratio = p01 * d0 * d0
            d1 = lax.rsqrt(p11 - ratio * p01)
            at = base + j
            u_ref[at : at + 1, :] = (r[j] * d0)[:1]
            u_ref[at + 1 : at + 2, :] = ((r[j + 1] - ratio * r[j]) * d1)[:1]
        if t0 + 1 == tiles:
            break
        for j in (4, 2, 0):
            for i in (j, j + 1):
                for k in range(j + 2, 8):
                    w[i] = w[i] - solved[i, k] * w[k]
        for t in range(t0 + 1, tiles):
            terms = [x[t][k] * w[k] for k in range(8)]
            a[t] = a[t] - (
                ((terms[0] + terms[1]) + (terms[2] + terms[3]))
                + ((terms[4] + terms[5]) + (terms[6] + terms[7]))
            )


def factor_block(d_ref, l_ref, z_ref, h_ref, u_ref):
    size = d_ref.shape[0]
    half = size // 2
    keep = lax.broadcasted_iota(jnp.int32, (half, half), 0) >= lax.broadcasted_iota(
        jnp.int32, (half, half), 1
    )
    empty = jnp.zeros((half, half), jnp.float32)
    factor_half(d_ref.at[:half, :], u_ref)
    z1 = halves(u_ref[:, half:])
    l_ref[:half, :half] = jnp.where(keep, u_ref[:, :half].T, 0.0)
    z_ref[:half, :half] = u_ref[:, half:]
    l21 = dot3(halves(d_ref[half:, :half]), z1, NT)
    part = halves(l21)
    h_ref[:, :half] = d_ref[half:, half:] - dot3(part, part, NT)
    l_ref[half:, :half] = l21
    l_ref[:half, half:] = empty
    z_ref[:half, half:] = empty
    cross = halves(dot3(part, z1, NN))
    factor_half(h_ref, u_ref)
    l_ref[half:, half:] = jnp.where(keep, u_ref[:, :half].T, 0.0)
    z_ref[half:, half:] = u_ref[:, half:]
    z_ref[half:, :half] = -dot3(halves(u_ref[:, half:]), cross, NN)


def cholesky_kernel(
    place, where_ref, blocks_ref, l_ref, z_ref, own_ref, a_ref, d_ref, f_ref, i_ref, h_ref, u_ref
):
    size = blocks_ref.shape[1]
    for j in range(KS):
        for i in range(j, KS):
            at = place(i, j)
            a_ref[i * size : (i + 1) * size, j * size : (j + 1) * size] = blocks_ref[
                at * size : (at + 1) * size, :
            ].astype(jnp.float32)
    d_ref[...] = a_ref[:size, :size]
    h_ref[...] = jnp.zeros_like(h_ref)

    def step(k, carry):
        factor_block(d_ref, f_ref, i_ref, h_ref, u_ref)
        begin = pl.multiple_of(k * size, size)
        z_ref[pl.ds(begin, size), :] = i_ref[...].astype(z_ref.dtype)

        @pl.when(where_ref[1] == k)
        def _():
            own_ref[...] = jnp.zeros_like(own_ref)
            own_ref[pl.ds(begin, size), :] = f_ref[...]

        for now in range(KS - 1):

            @pl.when(k == now)
            def _():
                low, high = now * size, (now + 1) * size
                panel = dot3(halves(a_ref[high:, low:high]), halves(i_ref[...]), NT)
                parts = halves(panel)
                l_ref[high:, low:high] = parts[0]

                @pl.when(where_ref[1] == now)
                def _():
                    own_ref[high:, :] = panel

                for j in range(now + 1, KS):
                    skip = (j - now - 1) * size
                    left = tuple(x[skip:] for x in parts)
                    right = tuple(x[skip : skip + size] for x in parts)
                    at = j * size
                    fresh = a_ref[at:, at : at + size] - dot3(left, right, NT)
                    if j == now + 1:
                        d_ref[...] = fresh[:size]
                    a_ref[at:, at : at + size] = fresh

        return carry

    lax.fori_loop(0, KS, step, 0)


def assemble_kernel(
    leaf_count, front_count, where_ref, map_ref, got_ref, front_ref,
    out_ref, piece_ref, across_ref, below_ref,
):
    children, spread, size, _ = got_ref.shape
    leaf_id, front_id = where_ref[0], where_ref[1]
    rows = out_ref.shape[1]
    for s in range(out_ref.shape[0]):
        out_ref[s] = front_ref[pl.ds(s, rows, stride=out_ref.shape[0]), :]
    for c in range(children):
        col = map_ref[c, front_id] // front_count
        for q in range(spread):
            at = pl.multiple_of(map_ref[c, leaf_id + leaf_count * q] // leaf_count * size, size)
            out_ref[col, pl.ds(at, size), :] += got_ref[c, q].astype(jnp.float32)
    top = piece_ref.shape[0]
    piece_ref[...] = out_ref[0, :top, :].astype(jnp.bfloat16)
    below_ref[...] = out_ref[0, top:, :].astype(jnp.bfloat16)
    for s in range(out_ref.shape[0]):
        across_ref[:, s * size : (s + 1) * size] = out_ref[s, :top, :].astype(jnp.bfloat16)


def solve_kernel(
    leaf_count, first, where_ref, l_ref, z_ref, own_ref, rows_ref, tops_ref, full_ref,
    out_ref, s_ref, w_ref,
):
    col_blocks, all_rows, size = full_ref.shape
    top = tops_ref.shape[0] // leaf_count // size
    rows = all_rows - top * size
    leaf_id, front_id = where_ref[0], where_ref[1]
    low = jnp.bfloat16
    for k in range(KS):
        at = slice(k * size, (k + 1) * size)
        inverse = z_ref[at, :]
        own = rows_ref[k * rows : (k + 1) * rows, :]
        distance = lax.rem(leaf_id - k % leaf_count + leaf_count, leaf_count)
        source = (distance * top + k // leaf_count) * size
        met = tops_ref[pl.ds(pl.multiple_of(source, size), size), first * size :]
        if k:
            before = l_ref[at, : k * size]
            own = (own.astype(jnp.float32) - dot(s_ref[:, : k * size], before, NT)).astype(low)
            met = (met.astype(jnp.float32) - dot(before, w_ref[: k * size, :], NN)).astype(low)
        solved = dot(own, inverse, NT)
        s_ref[:, at] = solved.astype(low)
        w_ref[at, :] = dot(inverse, met, NN).astype(low)

        @pl.when(front_id == k)
        def _():
            out_ref[pl.ds(top * size * col_blocks, rows, stride=col_blocks), :] = solved
            for t in range(top):
                from_row = pl.multiple_of((t * leaf_count + leaf_id) * size, size)
                out_ref[pl.ds(t * size * col_blocks, size, stride=col_blocks), :] = own_ref[
                    pl.ds(from_row, size), :
                ]

    def complement(s):
        chunk = 256 if rows % 256 == 0 else size
        for r in range(0, rows, chunk):
            left = s_ref[r : r + chunk, :]
            right = w_ref[:, (s - first) * size : (s - first + 1) * size]
            begin = top * size + r
            out_ref[pl.ds(begin * col_blocks + s, chunk, stride=col_blocks), :] = full_ref[
                s, begin : begin + chunk, :
            ] - dot(left, right, NN)
        out_ref[pl.ds(s, top * size, stride=col_blocks), :] = jnp.zeros(
            (top * size, size), jnp.float32
        )

    for s in range(first, col_blocks):
        if s == 0:
            pl.when(front_id >= KS)(functools.partial(complement, s))
        else:
            complement(s)


MESH = pl.DeviceIdType.MESH
DMA = pltpu.SemaphoreType.DMA


def ring_position(member, count):
    side = lax.rem(member, 2)
    step = lax.div(member, 2)
    return step + side * (count - 1 - 2 * step)


def ring_member(position, count):
    side = lax.div(position, count // 2)
    return 2 * (position + side * (count - 1 - 2 * position)) + side


def behind(position, steps, count):
    return lax.rem(position - steps + count, count)


def ring_hops(position, count, first, slot, sems):
    send, recv = sems
    half = count // 2
    rows = first.shape[0]
    after = ring_member(lax.rem(position + 1, count), count)
    ahead = ring_member(behind(position, 1, count), count)

    def hop(way, s):
        to = s if way == 0 else count - s
        source = first if s == 1 else slot(to - 1 if way == 0 else to + 1)
        target = slot(to)
        if s == half:
            part = pl.ds(0, rows // 2) if way == 0 else pl.ds(rows // 2, rows // 2)
            source, target = source.at[part], target.at[part]
        return pltpu.make_async_remote_copy(
            src_ref=source,
            dst_ref=target,
            send_sem=send.at[way, s],
            recv_sem=recv.at[way, s],
            device_id={"front": after if way == 0 else ahead},
            device_id_type=MESH,
        )

    return hop, (after, ahead)


def ring_run(hop, half, ready):
    for way in (0, 1):
        hop(way, 1).start()
    ready(0)
    for s in range(1, half + 1):
        for way in (0, 1):
            hop(way, s).wait_recv()
            if s < half:
                hop(way, s + 1).start()
        ready(s)
        if s < half:
            ready(2 * half - s)


def ring_end(hop, half):
    for s in range(1, half + 1):
        for way in (0, 1):
            hop(way, s).wait_send()


def greet(barrier, devices):
    for device in devices:
        pl.semaphore_signal(barrier, inc=1, device_id=device, device_id_type=MESH)
    pl.semaphore_wait(barrier, len(devices))


def update_kernel(
    leaf_count, front_count, panel_ref, blocks_ref, got_ref,
    slots, stage, land, ring_send, ring_recv, out_send, out_recv,
):
    leaf_id, front_id = lax.axis_index("leaf"), lax.axis_index("front")
    size = panel_ref.shape[0]
    half = front_count // 2
    position = ring_position(front_id, front_count)
    hop, beside = ring_hops(
        position, front_count, panel_ref, lambda s: slots.at[s], (ring_send, ring_recv)
    )
    greet(
        pltpu.get_barrier_semaphore(),
        [{"front": f} for f in beside]
        + [{"leaf": lax.rem(leaf_id + d, leaf_count)} for d in range(1, leaf_count)],
    )

    def deliver(s):
        block = ring_member(behind(position, s, front_count), front_count)
        owner, turn = lax.rem(block, leaf_count), lax.div(block, leaf_count)
        copy = pltpu.make_async_remote_copy(
            src_ref=stage.at[s],
            dst_ref=land.at[leaf_id, turn],
            send_sem=out_send.at[s],
            recv_sem=out_recv.at[leaf_id, turn],
            device_id={"leaf": owner},
            device_id_type=MESH,
        )
        return block, owner, turn, copy

    def ready(s):
        block, owner, turn, copy = deliver(s)
        rows = panel_ref[...] if s == 0 else slots[s]
        given = blocks_ref[pl.ds(pl.multiple_of(block * size, size), size), :]
        product = dot(rows, panel_ref[...], NT)
        value = (given.astype(jnp.float32) - product).astype(jnp.bfloat16)
        stage[s] = value

        @pl.when(owner == leaf_id)
        def _():
            land[leaf_id, turn] = value

        @pl.when(owner != leaf_id)
        def _():
            copy.start()

    ring_run(hop, half, ready)
    for d in range(1, leaf_count):
        source = lax.rem(leaf_id + d, leaf_count)
        for turn in range(land.shape[1]):
            pltpu.make_async_remote_copy(
                src_ref=stage.at[0],
                dst_ref=land.at[source, turn],
                send_sem=out_send.at[0],
                recv_sem=out_recv.at[source, turn],
                device_id={"leaf": source},
                device_id_type=MESH,
            ).wait_recv()
    got_ref[...] = land[...]
    for s in range(front_count):
        _, owner, _, copy = deliver(s)
        pl.when(owner != leaf_id)(copy.wait_send)
    ring_end(hop, half)


def corner_kernel(
    leaf_count, front_count, piece_ref, out_ref,
    held, ring_send, ring_recv, far_send, far_recv, near_send, near_recv,
):
    leaf_id, front_id = lax.axis_index("leaf"), lax.axis_index("front")
    rows = piece_ref.shape[0]
    half = front_count // 2
    chips = leaf_count // 2
    chip, core = lax.div(leaf_id, 2), lax.rem(leaf_id, 2)
    mate = leaf_id + 1 - 2 * core
    position = ring_position(front_id, front_count)
    hop, beside = ring_hops(
        position,
        front_count,
        piece_ref,
        lambda s: held.at[leaf_id, s],
        (ring_send, ring_recv),
    )
    greet(
        pltpu.get_barrier_semaphore(),
        [{"front": f} for f in beside]
        + [{"leaf": 2 * lax.rem(chip + d, chips) + core} for d in range(1, chips)]
        + [{"leaf": mate}],
    )

    def far(d, s, source):
        return pltpu.make_async_remote_copy(
            src_ref=held.at[source, s],
            dst_ref=held.at[source, s],
            send_sem=far_send.at[d - 1, s],
            recv_sem=far_recv.at[d - 1, s],
            device_id={"leaf": 2 * lax.rem(chip + d, chips) + core},
            device_id_type=MESH,
        )

    def near(d, s, source):
        return pltpu.make_async_remote_copy(
            src_ref=held.at[source, s],
            dst_ref=held.at[source, s],
            send_sem=near_send.at[d, s],
            recv_sem=near_recv.at[d, s],
            device_id={"leaf": mate},
            device_id_type=MESH,
        )

    held[leaf_id, 0] = piece_ref[...]

    def ready(s):
        for d in range(1, chips):
            far(d, s, leaf_id).start()
        near(0, s, leaf_id).start()

    ring_run(hop, half, ready)
    order = [0] + [t for s in range(1, half) for t in (s, front_count - s)] + [half]
    for s in order:
        for d in range(1, chips):
            source = 2 * behind(chip, d, chips) + core
            far(d, s, source).wait_recv()
            near(d, s, source).start()
    for s in order:
        for d in range(chips):
            near(d, s, 2 * behind(chip, d, chips) + 1 - core).wait_recv()
    for s in range(front_count):
        column = ring_member(behind(position, s, front_count), front_count)
        for source in range(leaf_count):
            at = pl.multiple_of((source * front_count + column) * rows, rows)
            out_ref[pl.ds(at, rows), :] = held[source, s]
    for s in range(front_count):
        for d in range(1, chips):
            far(d, s, leaf_id).wait_send()
        for d in range(chips):
            near(d, s, leaf_id).wait_send()
    ring_end(hop, half)


def gather_by_distance(x, axis):
    count = lax.axis_size(axis)
    pieces = [x]
    for d in range(1, count):
        pieces.append(lax.ppermute(x, axis, [(i, (i + d) % count) for i in range(count)]))
    return jnp.concatenate(pieces, axis=0)


def on_device(front_entries, child_panels, child_blocks, child_map):
    leaf_count = lax.axis_size("leaf")
    front_count = lax.axis_size("front")
    place = jnp.stack([lax.axis_index("leaf"), lax.axis_index("front")]).astype(jnp.int32)
    row_blocks, _, size, col_blocks, _, _ = front_entries.shape
    children = child_map.shape[0]
    spread = child_map.shape[1] // leaf_count
    rows = row_blocks * size
    top = KS // leaf_count
    first = KS // front_count
    params = pltpu.CompilerParams(vmem_limit_bytes=LIMIT)
    piv = child_panels.shape[2]
    half = front_count // 2
    ring = [DMA((2, half + 1)), DMA((2, half + 1))]
    got = pl.pallas_call(
        functools.partial(update_kernel, leaf_count, front_count),
        out_shape=jax.ShapeDtypeStruct((children, spread, size, size), jnp.bfloat16),
        in_specs=[VMEM, VMEM],
        out_specs=VMEM,
        scratch_shapes=[
            pltpu.VMEM((front_count, size, piv), jnp.bfloat16),
            pltpu.VMEM((front_count, size, size), jnp.bfloat16),
            pltpu.VMEM((children, spread, size, size), jnp.bfloat16),
        ]
        + ring
        + [DMA((front_count,)), DMA((children, spread))],
        compiler_params=pltpu.CompilerParams(
            vmem_limit_bytes=LIMIT, collective_id=0, has_side_effects=True
        ),
    )(child_panels[0], child_blocks[0])
    full, piece, across, below = pl.pallas_call(
        functools.partial(assemble_kernel, leaf_count, front_count),
        out_shape=[
            jax.ShapeDtypeStruct((col_blocks, rows, size), jnp.float32),
            jax.ShapeDtypeStruct((top * size, size), jnp.bfloat16),
            jax.ShapeDtypeStruct((top * size, col_blocks * size), jnp.bfloat16),
            jax.ShapeDtypeStruct((rows - top * size, size), jnp.bfloat16),
        ],
        in_specs=[SMEM, SMEM, VMEM, VMEM],
        out_specs=[VMEM] * 4,
        compiler_params=params,
    )(
        place,
        child_map,
        got,
        front_entries.reshape(rows * col_blocks, size),
    )
    chips = leaf_count // 2
    corner = pl.pallas_call(
        functools.partial(corner_kernel, leaf_count, front_count),
        out_shape=jax.ShapeDtypeStruct(
            (leaf_count * front_count * top * size, size), jnp.bfloat16
        ),
        in_specs=[VMEM],
        out_specs=VMEM,
        scratch_shapes=[pltpu.VMEM((leaf_count, front_count, top * size, size), jnp.bfloat16)]
        + ring
        + [DMA((max(chips - 1, 1), front_count))] * 2
        + [DMA((chips, front_count))] * 2,
        compiler_params=pltpu.CompilerParams(
            vmem_limit_bytes=LIMIT, collective_id=1, has_side_effects=True
        ),
    )(piece)
    corner, below, across = lax.optimization_barrier((corner, below, across))
    below = lax.all_gather(below, "front", axis=0, tiled=True)
    across = gather_by_distance(across, "leaf")
    width = KS * size

    def corner_place(i, j):
        return ((i % leaf_count) * front_count + j) * top + i // leaf_count

    lower, inverses, column = pl.pallas_call(
        functools.partial(cholesky_kernel, corner_place),
        out_shape=[
            jax.ShapeDtypeStruct((width, width), jnp.bfloat16),
            jax.ShapeDtypeStruct((width, size), jnp.bfloat16),
            jax.ShapeDtypeStruct((width, size), jnp.float32),
        ],
        in_specs=[SMEM, VMEM],
        out_specs=[VMEM] * 3,
        scratch_shapes=[pltpu.VMEM((width, width), jnp.float32)]
        + [pltpu.VMEM((size, size), jnp.float32)] * 3
        + [pltpu.VMEM((size // 2, size), jnp.float32)] * 2,
        compiler_params=params,
        cost_estimate=pl.CostEstimate(
            flops=8 * width**3, bytes_accessed=8 * width * width, transcendentals=0
        ),
    )(place, corner)
    result = pl.pallas_call(
        functools.partial(solve_kernel, leaf_count, first),
        out_shape=jax.ShapeDtypeStruct((rows * col_blocks, size), jnp.float32),
        in_specs=[SMEM] + [VMEM] * 6,
        out_specs=VMEM,
        scratch_shapes=[
            pltpu.VMEM((rows - top * size, width), jnp.bfloat16),
            pltpu.VMEM((width, (col_blocks - first) * size), jnp.bfloat16),
        ],
        compiler_params=params,
    )(place, lower, inverses, column, below, across, full)
    return result.reshape(row_blocks, 1, size, col_blocks, 1, size)


def solution(mesh):
    placed = (
        P(None, "leaf", None, None, "front", None),
        P("leaf", "front", None),
        P("leaf", None, "front"),
        P(),
    )
    return jax.shard_map(
        on_device,
        mesh=mesh,
        in_specs=placed,
        out_specs=P(None, "leaf", None, None, "front", None),
        check_vma=False,
    )
```

```python
import functools

import jax
import jax.numpy as jnp
from jax import lax
from jax.experimental import pallas as pl
from jax.experimental.pallas import tpu as pltpu
from jax.sharding import PartitionSpec as P

KS = 8
NT = (((1,), (1,)), ((), ()))
NN = (((1,), (0,)), ((), ()))
VMEM = pl.BlockSpec(memory_space=pltpu.VMEM)
SMEM = pl.BlockSpec(memory_space=pltpu.SMEM)
LIMIT = 56 * 1024 * 1024


def dot(a, b, dims):
    return lax.dot_general(a, b, dims, preferred_element_type=jnp.float32)


def halves(x):
    high = x.astype(jnp.bfloat16)
    return high, (x - high.astype(jnp.float32)).astype(jnp.bfloat16)


def dot3(a, b, dims):
    (ah, al), (bh, bl) = a, b
    left = jnp.concatenate([ah, ah, al], axis=1)
    right = jnp.concatenate([bh, bl, bh], axis=dims[0][1][0])
    return dot(left, right, dims)


def factor_half(a_ref, u_ref):
    size, width = a_ref.shape
    tiles = size // 8
    sub = lax.broadcasted_iota(jnp.int32, (8, width), 0)
    lane = lax.broadcasted_iota(jnp.int32, (8, width), 1)
    a = [
        jnp.where(
            lane < size,
            a_ref[8 * t : 8 * t + 8, :],
            jnp.where(lane == sub + (size + 8 * t), 1.0, 0.0),
        )
        for t in range(tiles)
    ]

    def row(tile, s):
        return jnp.broadcast_to(tile[s : s + 1, :], (8, width))

    def column(tile, j):
        return jnp.broadcast_to(tile[:, j : j + 1], (8, width))

    for t0 in range(tiles):
        base = 8 * t0
        spread = [column(a[t0], base + k) for k in range(8)]
        e = {(m, k): row(spread[k], m) for k in range(8) for m in range(k + 1)}
        r = [row(a[t0], m) for m in range(8)]
        x = {t: [column(a[t], base + k) for k in range(8)] for t in range(t0 + 1, tiles)}
        w, solved = [None] * 8, {}
        for j in range(0, 8, 2):
            p00, p01, p11 = e[j, j], e[j, j + 1], e[j + 1, j + 1]
            det = p00 * p11 - p01 * p01
            inv = pl.reciprocal(det, approx=True)
            inv = inv * (2.0 - det * inv)

            def pivot(first, second):
                return p11 * first - p01 * second, p00 * second - p01 * first

            raw = {}
            for m in range(j + 2, 8):
                raw[j, m], raw[j + 1, m] = pivot(e[j, m], e[j + 1, m])
                solved[j, m], solved[j + 1, m] = raw[j, m] * inv, raw[j + 1, m] * inv
            for m in range(j + 2, 8):
                for k in range(m, 8):
                    e[m, k] = e[m, k] - inv * (e[j, m] * raw[j, k] + e[j + 1, m] * raw[j + 1, k])
            w[j], w[j + 1] = pivot(r[j], r[j + 1])
            for m in range(j + 2, 8):
                r[m] = r[m] - inv * (e[j, m] * w[j] + e[j + 1, m] * w[j + 1])
            w[j], w[j + 1] = w[j] * inv, w[j + 1] * inv
            d0 = lax.rsqrt(p00)
            ratio = p01 * d0 * d0
            d1 = lax.rsqrt(p11 - ratio * p01)
            at = base + j
            u_ref[at : at + 1, :] = (r[j] * d0)[:1]
            u_ref[at + 1 : at + 2, :] = ((r[j + 1] - ratio * r[j]) * d1)[:1]
        if t0 + 1 == tiles:
            break
        for j in (4, 2, 0):
            for i in (j, j + 1):
                for k in range(7, j + 1, -1):
                    w[i] = w[i] - solved[i, k] * w[k]
        for t in range(t0 + 1, tiles):
            terms = [x[t][k] * w[k] for k in range(8)]
            a[t] = a[t] - (
                ((terms[0] + terms[1]) + (terms[2] + terms[3]))
                + ((terms[4] + terms[5]) + (terms[6] + terms[7]))
            )


def factor_block(d_ref, l_ref, z_ref, h_ref, u_ref):
    size = d_ref.shape[0]
    half = size // 2
    keep = lax.broadcasted_iota(jnp.int32, (half, half), 0) >= lax.broadcasted_iota(
        jnp.int32, (half, half), 1
    )
    empty = jnp.zeros((half, half), jnp.float32)
    factor_half(d_ref.at[:half, :], u_ref)
    z1 = halves(u_ref[:, half:])
    l_ref[:half, :half] = jnp.where(keep, u_ref[:, :half].T, 0.0)
    z_ref[:half, :half] = u_ref[:, half:]
    l21 = dot3(halves(d_ref[half:, :half]), z1, NT)
    part = halves(l21)
    h_ref[:, :half] = d_ref[half:, half:] - dot3(part, part, NT)
    l_ref[half:, :half] = l21
    l_ref[:half, half:] = empty
    z_ref[:half, half:] = empty
    cross = halves(dot3(part, z1, NN))
    factor_half(h_ref, u_ref)
    l_ref[half:, half:] = jnp.where(keep, u_ref[:, :half].T, 0.0)
    z_ref[half:, half:] = u_ref[:, half:]
    z_ref[half:, :half] = -dot3(halves(u_ref[:, half:]), cross, NN)


def cholesky_kernel(
    place, where_ref, blocks_ref, l_ref, z_ref, own_ref, a_ref, d_ref, f_ref, i_ref, h_ref, u_ref
):
    size = blocks_ref.shape[1]
    for j in range(KS):
        for i in range(j, KS):
            at = place(i, j)
            a_ref[i * size : (i + 1) * size, j * size : (j + 1) * size] = blocks_ref[
                at * size : (at + 1) * size, :
            ].astype(jnp.float32)
    d_ref[...] = a_ref[:size, :size]
    h_ref[...] = jnp.zeros_like(h_ref)

    def step(k, carry):
        factor_block(d_ref, f_ref, i_ref, h_ref, u_ref)
        begin = pl.multiple_of(k * size, size)
        z_ref[pl.ds(begin, size), :] = i_ref[...].astype(z_ref.dtype)

        @pl.when(where_ref[1] == k)
        def _():
            own_ref[...] = jnp.zeros_like(own_ref)
            own_ref[pl.ds(begin, size), :] = f_ref[...]

        for now in range(KS - 1):

            @pl.when(k == now)
            def _():
                low, high = now * size, (now + 1) * size
                panel = dot3(halves(a_ref[high:, low:high]), halves(i_ref[...]), NT)
                parts = halves(panel)
                l_ref[high:, low:high] = parts[0]

                @pl.when(where_ref[1] == now)
                def _():
                    own_ref[high:, :] = panel

                for j in range(now + 1, KS):
                    skip = (j - now - 1) * size
                    left = tuple(x[skip:] for x in parts)
                    right = tuple(x[skip : skip + size] for x in parts)
                    at = j * size
                    fresh = a_ref[at:, at : at + size] - dot3(left, right, NT)
                    if j == now + 1:
                        d_ref[...] = fresh[:size]
                    a_ref[at:, at : at + size] = fresh

        return carry

    lax.fori_loop(0, KS, step, 0)


def assemble_kernel(
    leaf_count, front_count, where_ref, map_ref, got_ref, front_ref,
    out_ref, piece_ref, across_ref, below_ref,
):
    children, spread, size, _ = got_ref.shape
    leaf_id, front_id = where_ref[0], where_ref[1]
    rows = out_ref.shape[1]
    for s in range(out_ref.shape[0]):
        out_ref[s] = front_ref[pl.ds(s, rows, stride=out_ref.shape[0]), :]
    for c in range(children):
        col = map_ref[c, front_id] // front_count
        for q in range(spread):
            at = pl.multiple_of(map_ref[c, leaf_id + leaf_count * q] // leaf_count * size, size)
            out_ref[col, pl.ds(at, size), :] += got_ref[c, q].astype(jnp.float32)
    top = piece_ref.shape[0]
    piece_ref[...] = out_ref[0, :top, :].astype(jnp.bfloat16)
    below_ref[...] = out_ref[0, top:, :].astype(jnp.bfloat16)
    for s in range(out_ref.shape[0]):
        across_ref[:, s * size : (s + 1) * size] = out_ref[s, :top, :].astype(jnp.bfloat16)


def solve_kernel(
    leaf_count, first, where_ref, l_ref, z_ref, own_ref, rows_ref, tops_ref, full_ref,
    out_ref, s_ref, w_ref,
):
    col_blocks, all_rows, size = full_ref.shape
    top = tops_ref.shape[0] // leaf_count // size
    rows = all_rows - top * size
    leaf_id, front_id = where_ref[0], where_ref[1]
    low = jnp.bfloat16
    for k in range(KS):
        at = slice(k * size, (k + 1) * size)
        inverse = z_ref[at, :]
        own = rows_ref[k * rows : (k + 1) * rows, :]
        distance = lax.rem(leaf_id - k % leaf_count + leaf_count, leaf_count)
        source = (distance * top + k // leaf_count) * size
        met = tops_ref[pl.ds(pl.multiple_of(source, size), size), first * size :]
        if k:
            before = l_ref[at, : k * size]
            own = (own.astype(jnp.float32) - dot(s_ref[:, : k * size], before, NT)).astype(low)
            met = (met.astype(jnp.float32) - dot(before, w_ref[: k * size, :], NN)).astype(low)
        solved = dot(own, inverse, NT)
        s_ref[:, at] = solved.astype(low)
        w_ref[at, :] = dot(inverse, met, NN).astype(low)

        @pl.when(front_id == k)
        def _():
            out_ref[pl.ds(top * size * col_blocks, rows, stride=col_blocks), :] = solved
            for t in range(top):
                from_row = pl.multiple_of((t * leaf_count + leaf_id) * size, size)
                out_ref[pl.ds(t * size * col_blocks, size, stride=col_blocks), :] = own_ref[
                    pl.ds(from_row, size), :
                ]

    def complement(s):
        chunk = 256 if rows % 256 == 0 else size
        for r in range(0, rows, chunk):
            left = s_ref[r : r + chunk, :]
            right = w_ref[:, (s - first) * size : (s - first + 1) * size]
            begin = top * size + r
            out_ref[pl.ds(begin * col_blocks + s, chunk, stride=col_blocks), :] = full_ref[
                s, begin : begin + chunk, :
            ] - dot(left, right, NN)
        out_ref[pl.ds(s, top * size, stride=col_blocks), :] = jnp.zeros(
            (top * size, size), jnp.float32
        )

    for s in range(first, col_blocks):
        if s == 0:
            pl.when(front_id >= KS)(functools.partial(complement, s))
        else:
            complement(s)


MESH = pl.DeviceIdType.MESH
DMA = pltpu.SemaphoreType.DMA


def ring_position(member, count):
    side = lax.rem(member, 2)
    step = lax.div(member, 2)
    return step + side * (count - 1 - 2 * step)


def ring_member(position, count):
    side = lax.div(position, count // 2)
    return 2 * (position + side * (count - 1 - 2 * position)) + side


def behind(position, steps, count):
    return lax.rem(position - steps + count, count)


def ring_hops(position, count, parts, first, slot, sems, need=None):
    send, recv = sems
    half = count // 2
    rows = first.shape[0] // parts
    after = ring_member(lax.rem(position + 1, count), count)
    ahead = ring_member(behind(position, 1, count), count)

    def act(kind, way, s, u):
        if s == half and (u < parts // 2) != (way == 0):
            return
        to = s if way == 0 else count - s
        before = to - 1 if way == 0 else to + 1
        part = pl.ds(u * rows, rows)
        copy = pltpu.make_async_remote_copy(
            src_ref=(first if s == 1 else slot(before)).at[part],
            dst_ref=slot(to).at[part],
            send_sem=send.at[way, s, u],
            recv_sem=recv.at[way, s, u],
            device_id={"front": after if way == 0 else ahead},
            device_id_type=MESH,
        )
        run = {"start": copy.start, "sent": copy.wait_send, "got": copy.wait_recv}[kind]
        if need is None:
            run()
        else:
            at = to if kind == "got" else before
            pl.when(need(u, ring_member(behind(position, at, count), count)))(run)

    return act, (after, ahead)


def ring_run(act, half, parts, ready):
    for u in range(parts):
        for way in (0, 1):
            act("start", way, 1, u)
    for u in range(parts):
        ready(0, u)
    for s in range(1, half + 1):
        for u in range(parts):
            for way in (0, 1):
                act("got", way, s, u)
                if s < half:
                    act("start", way, s + 1, u)
            ready(s, u)
            if s < half:
                ready(2 * half - s, u)


def ring_end(act, half, parts):
    for s in range(1, half + 1):
        for u in range(parts):
            for way in (0, 1):
                act("sent", way, s, u)


def greet(barrier, devices):
    for device in devices:
        pl.semaphore_signal(barrier, inc=1, device_id=device, device_id_type=MESH)
    pl.semaphore_wait(barrier, len(devices))


def update_kernel(
    leaf_count, front_count, panel_ref, blocks_ref, got_ref,
    slots, stage, land, ring_send, ring_recv, out_send, out_recv,
):
    leaf_id, front_id = lax.axis_index("leaf"), lax.axis_index("front")
    size = panel_ref.shape[0]
    half = front_count // 2
    position = ring_position(front_id, front_count)
    parts = ring_send.shape[2]
    act, beside = ring_hops(
        position, front_count, parts, panel_ref, lambda s: slots.at[s], (ring_send, ring_recv)
    )
    greet(
        pltpu.get_barrier_semaphore(),
        [{"front": f} for f in beside]
        + [{"leaf": lax.rem(leaf_id + d, leaf_count)} for d in range(1, leaf_count)],
    )

    def deliver(s):
        block = ring_member(behind(position, s, front_count), front_count)
        owner, turn = lax.rem(block, leaf_count), lax.div(block, leaf_count)
        copy = pltpu.make_async_remote_copy(
            src_ref=stage.at[s],
            dst_ref=land.at[leaf_id, turn],
            send_sem=out_send.at[s],
            recv_sem=out_recv.at[leaf_id, turn],
            device_id={"leaf": owner},
            device_id_type=MESH,
        )
        return block, owner, turn, copy

    def ready(s, u):
        if u + 1 < parts:
            return
        block, owner, turn, copy = deliver(s)
        rows = panel_ref[...] if s == 0 else slots[s]
        given = blocks_ref[pl.ds(pl.multiple_of(block * size, size), size), :]
        product = dot(rows, panel_ref[...], NT)
        value = (given.astype(jnp.float32) - product).astype(jnp.bfloat16)
        stage[s] = value

        @pl.when(owner == leaf_id)
        def _():
            land[leaf_id, turn] = value

        @pl.when(owner != leaf_id)
        def _():
            copy.start()

    ring_run(act, half, parts, ready)
    for d in range(1, leaf_count):
        source = lax.rem(leaf_id + d, leaf_count)
        for turn in range(land.shape[1]):
            pltpu.make_async_remote_copy(
                src_ref=stage.at[0],
                dst_ref=land.at[source, turn],
                send_sem=out_send.at[0],
                recv_sem=out_recv.at[source, turn],
                device_id={"leaf": source},
                device_id_type=MESH,
            ).wait_recv()
    got_ref[...] = land[...]
    for s in range(front_count):
        _, owner, _, copy = deliver(s)
        pl.when(owner != leaf_id)(copy.wait_send)
    ring_end(act, half, parts)


def corner_kernel(
    leaf_count, front_count, piece_ref, out_ref,
    held, ring_send, ring_recv, far_send, far_recv, near_send, near_recv,
):
    leaf_id, front_id = lax.axis_index("leaf"), lax.axis_index("front")
    rows, size = piece_ref.shape
    half = front_count // 2
    chips = leaf_count // 2
    chip, core = lax.div(leaf_id, 2), lax.rem(leaf_id, 2)
    mate = leaf_id + 1 - 2 * core
    position = ring_position(front_id, front_count)
    parts = ring_send.shape[2]
    blocks = rows // size
    unit = rows // parts

    def need(u, column, source=leaf_id):
        return u * blocks // parts * leaf_count + source >= column

    act, beside = ring_hops(
        position,
        front_count,
        parts,
        piece_ref,
        lambda s: held.at[leaf_id, s],
        (ring_send, ring_recv),
        need,
    )
    greet(
        pltpu.get_barrier_semaphore(),
        [{"front": f} for f in beside]
        + [{"leaf": 2 * lax.rem(chip + d, chips) + core} for d in range(1, chips)]
        + [{"leaf": mate}],
    )

    def pass_on(kind, d, s, u, source, near):
        part = held.at[source, s, pl.ds(u * unit, unit)]
        send, recv, at = (near_send, near_recv, d) if near else (far_send, far_recv, d - 1)
        copy = pltpu.make_async_remote_copy(
            src_ref=part,
            dst_ref=part,
            send_sem=send.at[at, s, u],
            recv_sem=recv.at[at, s, u],
            device_id={"leaf": mate if near else 2 * lax.rem(chip + d, chips) + core},
            device_id_type=MESH,
        )
        run = {"start": copy.start, "sent": copy.wait_send, "got": copy.wait_recv}[kind]
        column = ring_member(behind(position, s, front_count), front_count)
        pl.when(need(u, column, source))(run)

    held[leaf_id, 0] = piece_ref[...]

    def ready(s, u):
        for d in range(1, chips):
            pass_on("start", d, s, u, leaf_id, False)
        pass_on("start", 0, s, u, leaf_id, True)

    ring_run(act, half, parts, ready)
    order = [0] + [t for s in range(1, half) for t in (s, front_count - s)] + [half]
    for s in order:
        for u in range(parts):
            for d in range(1, chips):
                source = 2 * behind(chip, d, chips) + core
                pass_on("got", d, s, u, source, False)
                pass_on("start", d, s, u, source, True)
    for s in order:
        for u in range(parts):
            for d in range(chips):
                pass_on("got", d, s, u, 2 * behind(chip, d, chips) + 1 - core, True)
    for s in range(front_count):
        column = ring_member(behind(position, s, front_count), front_count)
        for source in range(leaf_count):
            for u in range(parts):

                @pl.when(need(u, column, source))
                def _():
                    at = pl.multiple_of((source * front_count + column) * rows + u * unit, unit)
                    out_ref[pl.ds(at, unit), :] = held[source, s, u * unit : (u + 1) * unit]

    for s in range(front_count):
        for u in range(parts):
            for d in range(1, chips):
                pass_on("sent", d, s, u, leaf_id, False)
            for d in range(chips):
                pass_on("sent", d, s, u, 2 * behind(chip, d, chips) + core, True)
    ring_end(act, half, parts)


def gather_by_distance(x, axis):
    count = lax.axis_size(axis)
    pieces = [x]
    for d in range(1, count):
        pieces.append(lax.ppermute(x, axis, [(i, (i + d) % count) for i in range(count)]))
    return jnp.concatenate(pieces, axis=0)


def on_device(front_entries, child_panels, child_blocks, child_map):
    leaf_count = lax.axis_size("leaf")
    front_count = lax.axis_size("front")
    place = jnp.stack([lax.axis_index("leaf"), lax.axis_index("front")]).astype(jnp.int32)
    row_blocks, _, size, col_blocks, _, _ = front_entries.shape
    children = child_map.shape[0]
    spread = child_map.shape[1] // leaf_count
    rows = row_blocks * size
    top = KS // leaf_count
    first = KS // front_count
    params = pltpu.CompilerParams(vmem_limit_bytes=LIMIT)
    piv = child_panels.shape[2]
    half = front_count // 2
    parts = max(top, 2)
    ring = [DMA((2, half + 1, parts))] * 2
    got = pl.pallas_call(
        functools.partial(update_kernel, leaf_count, front_count),
        out_shape=jax.ShapeDtypeStruct((children, spread, size, size), jnp.bfloat16),
        in_specs=[VMEM, VMEM],
        out_specs=VMEM,
        scratch_shapes=[
            pltpu.VMEM((front_count, size, piv), jnp.bfloat16),
            pltpu.VMEM((front_count, size, size), jnp.bfloat16),
            pltpu.VMEM((children, spread, size, size), jnp.bfloat16),
        ]
        + ring
        + [DMA((front_count,)), DMA((children, spread))],
        compiler_params=pltpu.CompilerParams(
            vmem_limit_bytes=LIMIT, collective_id=0, has_side_effects=True
        ),
    )(child_panels[0], child_blocks[0])
    full, piece, across, below = pl.pallas_call(
        functools.partial(assemble_kernel, leaf_count, front_count),
        out_shape=[
            jax.ShapeDtypeStruct((col_blocks, rows, size), jnp.float32),
            jax.ShapeDtypeStruct((top * size, size), jnp.bfloat16),
            jax.ShapeDtypeStruct((top * size, col_blocks * size), jnp.bfloat16),
            jax.ShapeDtypeStruct((rows - top * size, size), jnp.bfloat16),
        ],
        in_specs=[SMEM, SMEM, VMEM, VMEM],
        out_specs=[VMEM] * 4,
        compiler_params=params,
    )(
        place,
        child_map,
        got,
        front_entries.reshape(rows * col_blocks, size),
    )
    chips = leaf_count // 2
    corner = pl.pallas_call(
        functools.partial(corner_kernel, leaf_count, front_count),
        out_shape=jax.ShapeDtypeStruct(
            (leaf_count * front_count * top * size, size), jnp.bfloat16
        ),
        in_specs=[VMEM],
        out_specs=VMEM,
        scratch_shapes=[pltpu.VMEM((leaf_count, front_count, top * size, size), jnp.bfloat16)]
        + ring
        + [DMA((max(chips - 1, 1), front_count, parts))] * 2
        + [DMA((chips, front_count, parts))] * 2,
        compiler_params=pltpu.CompilerParams(
            vmem_limit_bytes=LIMIT, collective_id=1, has_side_effects=True
        ),
    )(piece)
    corner, below, across = lax.optimization_barrier((corner, below, across))
    below = lax.all_gather(below, "front", axis=0, tiled=True)
    across = gather_by_distance(across, "leaf")
    width = KS * size

    def corner_place(i, j):
        return ((i % leaf_count) * front_count + j) * top + i // leaf_count

    lower, inverses, column = pl.pallas_call(
        functools.partial(cholesky_kernel, corner_place),
        out_shape=[
            jax.ShapeDtypeStruct((width, width), jnp.bfloat16),
            jax.ShapeDtypeStruct((width, size), jnp.bfloat16),
            jax.ShapeDtypeStruct((width, size), jnp.float32),
        ],
        in_specs=[SMEM, VMEM],
        out_specs=[VMEM] * 3,
        scratch_shapes=[pltpu.VMEM((width, width), jnp.float32)]
        + [pltpu.VMEM((size, size), jnp.float32)] * 3
        + [pltpu.VMEM((size // 2, size), jnp.float32)] * 2,
        compiler_params=params,
        cost_estimate=pl.CostEstimate(
            flops=8 * width**3, bytes_accessed=8 * width * width, transcendentals=0
        ),
    )(place, corner)
    result = pl.pallas_call(
        functools.partial(solve_kernel, leaf_count, first),
        out_shape=jax.ShapeDtypeStruct((rows * col_blocks, size), jnp.float32),
        in_specs=[SMEM] + [VMEM] * 6,
        out_specs=VMEM,
        scratch_shapes=[
            pltpu.VMEM((rows - top * size, width), jnp.bfloat16),
            pltpu.VMEM((width, (col_blocks - first) * size), jnp.bfloat16),
        ],
        compiler_params=params,
    )(place, lower, inverses, column, below, across, full)
    return result.reshape(row_blocks, 1, size, col_blocks, 1, size)


def solution(mesh):
    placed = (
        P(None, "leaf", None, None, "front", None),
        P("leaf", "front", None),
        P("leaf", None, "front"),
        P(),
    )
    return jax.shard_map(
        on_device,
        mesh=mesh,
        in_specs=placed,
        out_specs=P(None, "leaf", None, None, "front", None),
        check_vma=False,
    )
```

```python
import functools

import jax
import jax.numpy as jnp
from jax import lax
from jax.experimental import pallas as pl
from jax.experimental.pallas import tpu as pltpu
from jax.sharding import PartitionSpec as P

KS = 8
NT = (((1,), (1,)), ((), ()))
NN = (((1,), (0,)), ((), ()))
VMEM = pl.BlockSpec(memory_space=pltpu.VMEM)
SMEM = pl.BlockSpec(memory_space=pltpu.SMEM)
LIMIT = 56 * 1024 * 1024


def dot(a, b, dims):
    return lax.dot_general(a, b, dims, preferred_element_type=jnp.float32)


def halves(x):
    high = x.astype(jnp.bfloat16)
    return high, (x - high.astype(jnp.float32)).astype(jnp.bfloat16)


def dot3(a, b, dims):
    (ah, al), (bh, bl) = a, b
    left = jnp.concatenate([ah, ah, al], axis=1)
    right = jnp.concatenate([bh, bl, bh], axis=dims[0][1][0])
    return dot(left, right, dims)


def factor_block(d_ref, u_ref, z_ref):
    size = d_ref.shape[0]
    tiles = size // 8
    sub = lax.broadcasted_iota(jnp.int32, (8, size), 0)
    lane = lax.broadcasted_iota(jnp.int32, (8, size), 1)
    a = [d_ref[8 * t : 8 * t + 8, :] for t in range(tiles)]
    z = [jnp.where(lane == sub + 8 * t, 1.0, 0.0).astype(jnp.float32) for t in range(tiles)]

    def row(tile, s):
        return jnp.broadcast_to(tile[s : s + 1, :], (8, size))

    def column(tile, j):
        return jnp.broadcast_to(tile[:, j : j + 1], (8, size))

    def total(x, w):
        terms = [x[k] * w[k] for k in range(8)]
        return ((terms[0] + terms[1]) + (terms[2] + terms[3])) + (
            (terms[4] + terms[5]) + (terms[6] + terms[7])
        )

    for t0 in range(tiles):
        base = 8 * t0
        spread = [column(a[t0], base + k) for k in range(8)]
        e = {(m, k): row(spread[k], m) for k in range(8) for m in range(k + 1)}
        sides = [[row(a[t0], m) for m in range(8)], [row(z[t0], m) for m in range(8)]]
        x = {t: [column(a[t], base + k) for k in range(8)] for t in range(t0 + 1, tiles)}
        both, solved = [[None] * 8, [None] * 8], {}
        for j in range(0, 8, 2):
            p00, p01, p11 = e[j, j], e[j, j + 1], e[j + 1, j + 1]
            det = p00 * p11 - p01 * p01
            inv = pl.reciprocal(det, approx=True)
            inv = inv * (2.0 - det * inv)

            def pivot(first, second):
                return p11 * first - p01 * second, p00 * second - p01 * first

            raw = {}
            for m in range(j + 2, 8):
                raw[j, m], raw[j + 1, m] = pivot(e[j, m], e[j + 1, m])
                solved[j, m], solved[j + 1, m] = raw[j, m] * inv, raw[j + 1, m] * inv
            for m in range(j + 2, 8):
                for k in range(m, 8):
                    e[m, k] = e[m, k] - inv * (e[j, m] * raw[j, k] + e[j + 1, m] * raw[j + 1, k])
            d0 = lax.rsqrt(p00)
            ratio = p01 * d0 * d0
            d1 = lax.rsqrt(p11 - ratio * p01)
            at = base + j
            for r, w, out_ref in zip(sides, both, (u_ref, z_ref)):
                first, second = pivot(r[j], r[j + 1])
                w[j], w[j + 1] = first * inv, second * inv
                for m in range(j + 2, 8):
                    r[m] = r[m] - (e[j, m] * w[j] + e[j + 1, m] * w[j + 1])
                out_ref[at : at + 1, :] = (r[j] * d0)[:1]
                out_ref[at + 1 : at + 2, :] = ((r[j + 1] - ratio * r[j]) * d1)[:1]
        if t0 + 1 == tiles:
            break
        for w in both:
            for j in (4, 2, 0):
                for i in (j, j + 1):
                    for k in range(7, j + 1, -1):
                        w[i] = w[i] - solved[i, k] * w[k]
        for t in range(t0 + 1, tiles):
            a[t] = a[t] - total(x[t], both[0])
            z[t] = z[t] - total(x[t], both[1])


def cholesky_kernel(
    place, where_ref, blocks_ref, l_ref, z_ref, own_ref, a_ref, d_ref, u_ref, i_ref
):
    size = blocks_ref.shape[1]
    for j in range(KS):
        for i in range(j, KS):
            at = place(i, j)
            a_ref[i * size : (i + 1) * size, j * size : (j + 1) * size] = blocks_ref[
                at * size : (at + 1) * size, :
            ].astype(jnp.float32)
    d_ref[...] = a_ref[:size, :size]
    keep = lax.broadcasted_iota(jnp.int32, (size, size), 0) >= lax.broadcasted_iota(
        jnp.int32, (size, size), 1
    )

    def step(k, carry):
        factor_block(d_ref, u_ref, i_ref)
        begin = pl.multiple_of(k * size, size)
        z_ref[pl.ds(begin, size), :] = i_ref[...].astype(z_ref.dtype)

        @pl.when(where_ref[1] == k)
        def _():
            own_ref[...] = jnp.zeros_like(own_ref)
            own_ref[pl.ds(begin, size), :] = jnp.where(keep, u_ref[...].T, 0.0)

        for now in range(KS - 1):

            @pl.when(k == now)
            def _():
                low, high = now * size, (now + 1) * size
                panel = dot3(halves(a_ref[high:, low:high]), halves(i_ref[...]), NT)
                rounded = panel.astype(jnp.bfloat16)
                l_ref[high:, low:high] = rounded

                @pl.when(where_ref[1] == now)
                def _():
                    own_ref[high:, :] = panel

                for j in range(now + 1, KS):
                    skip = (j - now - 1) * size
                    at = j * size
                    fresh = a_ref[at:, at : at + size] - dot(
                        rounded[skip:], rounded[skip : skip + size], NT
                    )
                    if j == now + 1:
                        d_ref[...] = fresh[:size]
                    a_ref[at:, at : at + size] = fresh

        return carry

    lax.fori_loop(0, KS, step, 0)


def assemble_kernel(
    leaf_count, front_count, where_ref, map_ref, got_ref, front_ref,
    out_ref, piece_ref, across_ref, below_ref,
):
    children, spread, size, _ = got_ref.shape
    leaf_id, front_id = where_ref[0], where_ref[1]
    rows = out_ref.shape[1]
    for s in range(out_ref.shape[0]):
        out_ref[s] = front_ref[pl.ds(s, rows, stride=out_ref.shape[0]), :]
    for c in range(children):
        col = map_ref[c, front_id] // front_count
        for q in range(spread):
            at = pl.multiple_of(map_ref[c, leaf_id + leaf_count * q] // leaf_count * size, size)
            out_ref[col, pl.ds(at, size), :] += got_ref[c, q].astype(jnp.float32)
    top = piece_ref.shape[0]
    piece_ref[...] = out_ref[0, :top, :].astype(jnp.bfloat16)
    below_ref[...] = out_ref[0, top:, :].astype(jnp.bfloat16)
    for s in range(out_ref.shape[0]):
        across_ref[:, s * size : (s + 1) * size] = out_ref[s, :top, :].astype(jnp.bfloat16)


def solve_kernel(
    leaf_count, first, where_ref, l_ref, z_ref, own_ref, rows_ref, tops_ref, full_ref,
    out_ref, s_ref, w_ref,
):
    col_blocks, all_rows, size = full_ref.shape
    top = tops_ref.shape[0] // leaf_count // size
    rows = all_rows - top * size
    leaf_id, front_id = where_ref[0], where_ref[1]
    low = jnp.bfloat16
    for k in range(KS):
        at = slice(k * size, (k + 1) * size)
        inverse = z_ref[at, :]
        own = rows_ref[k * rows : (k + 1) * rows, :]
        distance = lax.rem(leaf_id - k % leaf_count + leaf_count, leaf_count)
        source = (distance * top + k // leaf_count) * size
        met = tops_ref[pl.ds(pl.multiple_of(source, size), size), first * size :]
        if k:
            before = l_ref[at, : k * size]
            own = (own.astype(jnp.float32) - dot(s_ref[:, : k * size], before, NT)).astype(low)
            met = (met.astype(jnp.float32) - dot(before, w_ref[: k * size, :], NN)).astype(low)
        solved = dot(own, inverse, NT)
        s_ref[:, at] = solved.astype(low)
        w_ref[at, :] = dot(inverse, met, NN).astype(low)

        @pl.when(front_id == k)
        def _():
            out_ref[pl.ds(top * size * col_blocks, rows, stride=col_blocks), :] = solved
            for t in range(top):
                from_row = pl.multiple_of((t * leaf_count + leaf_id) * size, size)
                out_ref[pl.ds(t * size * col_blocks, size, stride=col_blocks), :] = own_ref[
                    pl.ds(from_row, size), :
                ]

    def complement(s):
        chunk = 256 if rows % 256 == 0 else size
        for r in range(0, rows, chunk):
            left = s_ref[r : r + chunk, :]
            right = w_ref[:, (s - first) * size : (s - first + 1) * size]
            begin = top * size + r
            out_ref[pl.ds(begin * col_blocks + s, chunk, stride=col_blocks), :] = full_ref[
                s, begin : begin + chunk, :
            ] - dot(left, right, NN)
        out_ref[pl.ds(s, top * size, stride=col_blocks), :] = jnp.zeros(
            (top * size, size), jnp.float32
        )

    for s in range(first, col_blocks):
        if s == 0:
            pl.when(front_id >= KS)(functools.partial(complement, s))
        else:
            complement(s)


MESH = pl.DeviceIdType.MESH
DMA = pltpu.SemaphoreType.DMA


def ring_position(member, count):
    side = lax.rem(member, 2)
    step = lax.div(member, 2)
    return step + side * (count - 1 - 2 * step)


def ring_member(position, count):
    side = lax.div(position, count // 2)
    return 2 * (position + side * (count - 1 - 2 * position)) + side


def behind(position, steps, count):
    return lax.rem(position - steps + count, count)


def ring_hops(position, count, parts, first, slot, sems, need=None):
    send, recv = sems
    half = count // 2
    rows = first.shape[0] // parts
    after = ring_member(lax.rem(position + 1, count), count)
    ahead = ring_member(behind(position, 1, count), count)

    def act(kind, way, s, u):
        if s == half and (u < parts // 2) != (way == 0):
            return
        to = s if way == 0 else count - s
        before = to - 1 if way == 0 else to + 1
        part = pl.ds(u * rows, rows)
        copy = pltpu.make_async_remote_copy(
            src_ref=(first if s == 1 else slot(before)).at[part],
            dst_ref=slot(to).at[part],
            send_sem=send.at[way, s, u],
            recv_sem=recv.at[way, s, u],
            device_id={"front": after if way == 0 else ahead},
            device_id_type=MESH,
        )
        run = {"start": copy.start, "sent": copy.wait_send, "got": copy.wait_recv}[kind]
        if need is None:
            run()
        else:
            at = to if kind == "got" else before
            pl.when(need(u, ring_member(behind(position, at, count), count)))(run)

    return act, (after, ahead)


def ring_run(act, half, parts, ready):
    for u in range(parts):
        for way in (0, 1):
            act("start", way, 1, u)
    for u in range(parts):
        ready(0, u)
    for s in range(1, half + 1):
        for u in range(parts):
            for way in (0, 1):
                act("got", way, s, u)
                if s < half:
                    act("start", way, s + 1, u)
            ready(s, u)
            if s < half:
                ready(2 * half - s, u)


def ring_end(act, half, parts):
    for s in range(1, half + 1):
        for u in range(parts):
            for way in (0, 1):
                act("sent", way, s, u)


def greet(barrier, devices):
    for device in devices:
        pl.semaphore_signal(barrier, inc=1, device_id=device, device_id_type=MESH)
    pl.semaphore_wait(barrier, len(devices))


def update_kernel(
    leaf_count, front_count, panel_ref, blocks_ref, got_ref,
    slots, stage, land, ring_send, ring_recv, out_send, out_recv,
):
    leaf_id, front_id = lax.axis_index("leaf"), lax.axis_index("front")
    size = panel_ref.shape[0]
    half = front_count // 2
    position = ring_position(front_id, front_count)
    parts = ring_send.shape[2]
    act, beside = ring_hops(
        position, front_count, parts, panel_ref, lambda s: slots.at[s], (ring_send, ring_recv)
    )
    greet(
        pltpu.get_barrier_semaphore(),
        [{"front": f} for f in beside]
        + [{"leaf": lax.rem(leaf_id + d, leaf_count)} for d in range(1, leaf_count)],
    )

    def deliver(s):
        block = ring_member(behind(position, s, front_count), front_count)
        owner, turn = lax.rem(block, leaf_count), lax.div(block, leaf_count)
        copy = pltpu.make_async_remote_copy(
            src_ref=stage.at[s],
            dst_ref=land.at[leaf_id, turn],
            send_sem=out_send.at[s],
            recv_sem=out_recv.at[leaf_id, turn],
            device_id={"leaf": owner},
            device_id_type=MESH,
        )
        return block, owner, turn, copy

    def ready(s, u):
        if u + 1 < parts:
            return
        block, owner, turn, copy = deliver(s)
        rows = panel_ref[...] if s == 0 else slots[s]
        given = blocks_ref[pl.ds(pl.multiple_of(block * size, size), size), :]
        product = dot(rows, panel_ref[...], NT)
        value = (given.astype(jnp.float32) - product).astype(jnp.bfloat16)
        stage[s] = value

        @pl.when(owner == leaf_id)
        def _():
            land[leaf_id, turn] = value

        @pl.when(owner != leaf_id)
        def _():
            copy.start()

    ring_run(act, half, parts, ready)
    for d in range(1, leaf_count):
        source = lax.rem(leaf_id + d, leaf_count)
        for turn in range(land.shape[1]):
            pltpu.make_async_remote_copy(
                src_ref=stage.at[0],
                dst_ref=land.at[source, turn],
                send_sem=out_send.at[0],
                recv_sem=out_recv.at[source, turn],
                device_id={"leaf": source},
                device_id_type=MESH,
            ).wait_recv()
    got_ref[...] = land[...]
    for s in range(front_count):
        _, owner, _, copy = deliver(s)
        pl.when(owner != leaf_id)(copy.wait_send)
    ring_end(act, half, parts)


def corner_kernel(
    leaf_count, front_count, piece_ref, out_ref,
    held, ring_send, ring_recv, far_send, far_recv, near_send, near_recv,
):
    leaf_id, front_id = lax.axis_index("leaf"), lax.axis_index("front")
    rows, size = piece_ref.shape
    half = front_count // 2
    chips = leaf_count // 2
    chip, core = lax.div(leaf_id, 2), lax.rem(leaf_id, 2)
    mate = leaf_id + 1 - 2 * core
    position = ring_position(front_id, front_count)
    parts = ring_send.shape[2]
    blocks = rows // size
    unit = rows // parts

    def need(u, column, source=leaf_id):
        return u * blocks // parts * leaf_count + source >= column

    act, beside = ring_hops(
        position,
        front_count,
        parts,
        piece_ref,
        lambda s: held.at[leaf_id, s],
        (ring_send, ring_recv),
        need,
    )
    greet(
        pltpu.get_barrier_semaphore(),
        [{"front": f} for f in beside]
        + [{"leaf": 2 * lax.rem(chip + d, chips) + core} for d in range(1, chips)]
        + [{"leaf": mate}],
    )

    def pass_on(kind, d, s, u, source, near):
        part = held.at[source, s, pl.ds(u * unit, unit)]
        send, recv, at = (near_send, near_recv, d) if near else (far_send, far_recv, d - 1)
        copy = pltpu.make_async_remote_copy(
            src_ref=part,
            dst_ref=part,
            send_sem=send.at[at, s, u],
            recv_sem=recv.at[at, s, u],
            device_id={"leaf": mate if near else 2 * lax.rem(chip + d, chips) + core},
            device_id_type=MESH,
        )
        run = {"start": copy.start, "sent": copy.wait_send, "got": copy.wait_recv}[kind]
        column = ring_member(behind(position, s, front_count), front_count)
        pl.when(need(u, column, source))(run)

    held[leaf_id, 0] = piece_ref[...]

    def ready(s, u):
        for d in range(1, chips):
            pass_on("start", d, s, u, leaf_id, False)
        pass_on("start", 0, s, u, leaf_id, True)

    ring_run(act, half, parts, ready)
    order = [0] + [t for s in range(1, half) for t in (s, front_count - s)] + [half]
    for s in order:
        for u in range(parts):
            for d in range(1, chips):
                source = 2 * behind(chip, d, chips) + core
                pass_on("got", d, s, u, source, False)
                pass_on("start", d, s, u, source, True)
    for s in order:
        for u in range(parts):
            for d in range(chips):
                pass_on("got", d, s, u, 2 * behind(chip, d, chips) + 1 - core, True)
    for s in range(front_count):
        column = ring_member(behind(position, s, front_count), front_count)
        for source in range(leaf_count):
            for u in range(parts):

                @pl.when(need(u, column, source))
                def _():
                    at = pl.multiple_of((source * front_count + column) * rows + u * unit, unit)
                    out_ref[pl.ds(at, unit), :] = held[source, s, u * unit : (u + 1) * unit]

    for s in range(front_count):
        for u in range(parts):
            for d in range(1, chips):
                pass_on("sent", d, s, u, leaf_id, False)
            for d in range(chips):
                pass_on("sent", d, s, u, 2 * behind(chip, d, chips) + core, True)
    ring_end(act, half, parts)


def gather_by_distance(x, axis):
    count = lax.axis_size(axis)
    pieces = [x]
    for d in range(1, count):
        pieces.append(lax.ppermute(x, axis, [(i, (i + d) % count) for i in range(count)]))
    return jnp.concatenate(pieces, axis=0)


def on_device(front_entries, child_panels, child_blocks, child_map):
    leaf_count = lax.axis_size("leaf")
    front_count = lax.axis_size("front")
    place = jnp.stack([lax.axis_index("leaf"), lax.axis_index("front")]).astype(jnp.int32)
    row_blocks, _, size, col_blocks, _, _ = front_entries.shape
    children = child_map.shape[0]
    spread = child_map.shape[1] // leaf_count
    rows = row_blocks * size
    top = KS // leaf_count
    first = KS // front_count
    params = pltpu.CompilerParams(vmem_limit_bytes=LIMIT)
    piv = child_panels.shape[2]
    half = front_count // 2
    parts = max(top, 2)
    ring = [DMA((2, half + 1, parts))] * 2
    got = pl.pallas_call(
        functools.partial(update_kernel, leaf_count, front_count),
        out_shape=jax.ShapeDtypeStruct((children, spread, size, size), jnp.bfloat16),
        in_specs=[VMEM, VMEM],
        out_specs=VMEM,
        scratch_shapes=[
            pltpu.VMEM((front_count, size, piv), jnp.bfloat16),
            pltpu.VMEM((front_count, size, size), jnp.bfloat16),
            pltpu.VMEM((children, spread, size, size), jnp.bfloat16),
        ]
        + ring
        + [DMA((front_count,)), DMA((children, spread))],
        compiler_params=pltpu.CompilerParams(
            vmem_limit_bytes=LIMIT, collective_id=0, has_side_effects=True
        ),
    )(child_panels[0], child_blocks[0])
    full, piece, across, below = pl.pallas_call(
        functools.partial(assemble_kernel, leaf_count, front_count),
        out_shape=[
            jax.ShapeDtypeStruct((col_blocks, rows, size), jnp.float32),
            jax.ShapeDtypeStruct((top * size, size), jnp.bfloat16),
            jax.ShapeDtypeStruct((top * size, col_blocks * size), jnp.bfloat16),
            jax.ShapeDtypeStruct((rows - top * size, size), jnp.bfloat16),
        ],
        in_specs=[SMEM, SMEM, VMEM, VMEM],
        out_specs=[VMEM] * 4,
        compiler_params=params,
    )(
        place,
        child_map,
        got,
        front_entries.reshape(rows * col_blocks, size),
    )
    chips = leaf_count // 2
    corner = pl.pallas_call(
        functools.partial(corner_kernel, leaf_count, front_count),
        out_shape=jax.ShapeDtypeStruct(
            (leaf_count * front_count * top * size, size), jnp.bfloat16
        ),
        in_specs=[VMEM],
        out_specs=VMEM,
        scratch_shapes=[pltpu.VMEM((leaf_count, front_count, top * size, size), jnp.bfloat16)]
        + ring
        + [DMA((max(chips - 1, 1), front_count, parts))] * 2
        + [DMA((chips, front_count, parts))] * 2,
        compiler_params=pltpu.CompilerParams(
            vmem_limit_bytes=LIMIT, collective_id=1, has_side_effects=True
        ),
    )(piece)
    corner, below, across = lax.optimization_barrier((corner, below, across))
    below = lax.all_gather(below, "front", axis=0, tiled=True)
    across = gather_by_distance(across, "leaf")
    width = KS * size

    def corner_place(i, j):
        return ((i % leaf_count) * front_count + j) * top + i // leaf_count

    lower, inverses, column = pl.pallas_call(
        functools.partial(cholesky_kernel, corner_place),
        out_shape=[
            jax.ShapeDtypeStruct((width, width), jnp.bfloat16),
            jax.ShapeDtypeStruct((width, size), jnp.bfloat16),
            jax.ShapeDtypeStruct((width, size), jnp.float32),
        ],
        in_specs=[SMEM, VMEM],
        out_specs=[VMEM] * 3,
        scratch_shapes=[pltpu.VMEM((width, width), jnp.float32)]
        + [pltpu.VMEM((size, size), jnp.float32)] * 3,
        compiler_params=params,
        cost_estimate=pl.CostEstimate(
            flops=8 * width**3, bytes_accessed=8 * width * width, transcendentals=0
        ),
    )(place, corner)
    result = pl.pallas_call(
        functools.partial(solve_kernel, leaf_count, first),
        out_shape=jax.ShapeDtypeStruct((rows * col_blocks, size), jnp.float32),
        in_specs=[SMEM] + [VMEM] * 6,
        out_specs=VMEM,
        scratch_shapes=[
            pltpu.VMEM((rows - top * size, width), jnp.bfloat16),
            pltpu.VMEM((width, (col_blocks - first) * size), jnp.bfloat16),
        ],
        compiler_params=params,
    )(place, lower, inverses, column, below, across, full)
    return result.reshape(row_blocks, 1, size, col_blocks, 1, size)


def solution(mesh):
    placed = (
        P(None, "leaf", None, None, "front", None),
        P("leaf", "front", None),
        P("leaf", None, "front"),
        P(),
    )
    return jax.shard_map(
        on_device,
        mesh=mesh,
        in_specs=placed,
        out_specs=P(None, "leaf", None, None, "front", None),
        check_vma=False,
    )
```
